256 devices in a mesh: replica: 4 (over y), shard: 64 (over z, x, core).
Axes of the slice: x: 4, y: 4, z: 8, core: 2. Of those that a mesh axis runs over, the one named last changes fastest.
Arguments:
- grads: bfloat16 [4, 32, 512, 3584], P('replica', None, 'shard')
- owner_table: int32 [4, 64], replicated, may hold values from 0 to 63, each once within a row
- momentum: float32 [4, 64, 512, 512], P('replica', 'shard'), may hold values from -6 to 6
- second: float32 [4, 64, 512, 512], P('replica', 'shard'), may hold values from 0.01 to 1
- left_stat: float32 [4, 64, 512, 512], P('replica', 'shard')
- right_stat: float32 [4, 64, 512, 512], P('replica', 'shard')
- left_root: float32 [4, 64, 512, 512], P('replica', 'shard')
- right_root: float32 [4, 64, 512, 512], P('replica', 'shard')
Outputs:
- update: bfloat16 [32, 512, 3584], P(None, 'shard', 'replica')
- momentum_out: float32 [4, 64, 512, 512], P('replica', 'shard')
- second_out: float32 [4, 64, 512, 512], P('replica', 'shard')
- left_out: float32 [4, 64, 512, 512], P('replica', 'shard')
- right_out: float32 [4, 64, 512, 512], P('replica', 'shard')
The draws below stay inside these ranges and needn't reach their ends.
Inputs may be any that keep to these rules, and one draw needn't show every extreme that they name: Each row of owner_table names every device index 0 to 63 once.
All inputs are finite; a program needn't handle non-finite values.
Results may differ from the reference program's by a relative error of at most 0.014.
Values may be sent and summed in bfloat16 or wider, within the bound.
A program may use at most 64 MiB of HBM per device.

```python
import math
import jax
import jax.numpy as jnp
from jax import lax

D = 3584
BLOCK = 512
QW = 896
CBQ = 2
RB = 32
NB = 64
N_REPLICA = 4
N_SHARD = 64


def dominant_block(key, diag_lo, diag_hi, spread):
    key_diag, key_jitter = jax.random.split(key)
    diagonal = jnp.exp(jax.random.uniform(key_diag, (N_REPLICA, N_SHARD, BLOCK), jnp.float32, math.log(diag_lo), math.log(diag_hi)))
    jitter = jax.random.normal(key_jitter, (N_REPLICA, N_SHARD, BLOCK, BLOCK), jnp.float32) * spread
    symmetric = 0.5 * (jitter + jnp.swapaxes(jitter, -1, -2))
    identity = jnp.eye(BLOCK, dtype=jnp.float32)
    return symmetric * (1.0 - identity) + identity * diagonal[..., None]


def draw_grads(key, part):
    key = jax.random.fold_in(key, 11)
    key_rows, key_cols, key_own = jax.random.split(key, 3)
    row_scale = jnp.exp(jax.random.uniform(key_rows, (1, RB, BLOCK, 1), jnp.float32, 0.0, math.log(10.0)))
    col_scale = jnp.exp(jax.random.uniform(key_cols, (1, 1, 1, D), jnp.float32, 0.0, math.log(10.0)))
    jitter = jax.random.normal(key_own, (N_REPLICA, RB, BLOCK, D), jnp.float32)
    return (0.005 * row_scale * col_scale * jitter).astype(jnp.bfloat16)


def draw_left_stat(key, part):
    key = jax.random.fold_in(key, 21)
    return dominant_block(key, 1.0, 10.0, 0.05)


def draw_right_stat(key, part):
    key = jax.random.fold_in(key, 22)
    return dominant_block(key, 1.0, 10.0, 0.05)


def draw_left_root(key, part):
    key = jax.random.fold_in(key, 23)
    return dominant_block(key, 0.5, 1.5, 0.02)


def draw_right_root(key, part):
    key = jax.random.fold_in(key, 24)
    return dominant_block(key, 0.5, 1.5, 0.02)


def block_levels(own_key, shape, cuts, least, top_value):
    gain, own = 1.0, jax.random.fold_in(own_key, 6)
    for axis_at, parts in cuts:
        heights = jnp.exp(jax.random.uniform(jax.random.fold_in(own, axis_at), (parts,), jnp.float32, least / len(cuts), top_value / len(cuts)))
        gain = gain * jnp.repeat(heights, shape[axis_at] // parts).reshape([-1 if axis == axis_at else 1 for axis in range(len(shape))])
    return gain


def scatter_about(own_key, dims, deviation, reach, pieces=(), held_as=jnp.bfloat16):
    factor_of = block_levels(own_key, dims, pieces, -0.22, 0.18) if pieces else 1.0
    drawn = jax.random.normal(own_key, dims, jnp.float32) * deviation * factor_of
    return jnp.minimum(jnp.maximum(drawn, -reach), reach).astype(held_as)


def setup_inputs(seed: int = 0) -> dict:
    key_of = jax.random.split(jax.random.key(seed), 9)
    return {
        "grads": draw_grads(jax.random.fold_in(key_of[8], 71), 0),
        "owner_table": jax.vmap(lambda own: jax.random.permutation(own, NB))(jax.random.split(key_of[1], N_REPLICA)).reshape((N_REPLICA, NB)).astype(jnp.int32),
        "momentum": scatter_about(key_of[2], (N_REPLICA, N_SHARD, BLOCK, BLOCK), 1.0, 6.0, ((0, 4), (1, 64)), jnp.float32),
        "second": jnp.clip(jnp.exp(math.log(1.0) - 4.6051702 * jax.random.uniform(key_of[3], (N_REPLICA, N_SHARD, BLOCK, BLOCK), jnp.float32) ** block_levels(key_of[3], (N_REPLICA, N_SHARD, BLOCK, BLOCK), ((0, 4), (1, 64)), -0.2, 0.2)), 0.01, 1.0),
        "left_stat": draw_left_stat(jax.random.fold_in(key_of[8], 71), 0),
        "right_stat": draw_right_stat(jax.random.fold_in(key_of[8], 71), 0),
        "left_root": draw_left_root(jax.random.fold_in(key_of[8], 71), 0),
        "right_root": draw_right_root(jax.random.fold_in(key_of[8], 71), 0),
    }


BETA_STAT = 0.95
BETA_SECOND = 0.99
BETA_MOMENT = 0.9
EPS_ADAM = 1e-08
EPS_NORM = 1e-06
LEARN_RATE = 0.5
HIGHEST = lax.Precision.HIGHEST

def owner_update(grad_block, col_mask, left_stat, right_stat, left_root, right_root, moment, second):
    gram_left = jnp.dot(grad_block, grad_block.T, precision=HIGHEST)
    gram_right = jnp.dot(grad_block.T, grad_block, precision=HIGHEST)
    left_new = BETA_STAT * left_stat + (1.0 - BETA_STAT) * gram_left
    right_new = BETA_STAT * right_stat + (1.0 - BETA_STAT) * gram_right
    second_new = BETA_SECOND * second + (1.0 - BETA_SECOND) * grad_block * grad_block
    adam_dir = col_mask * grad_block / (jnp.sqrt(second_new) + EPS_ADAM)
    shaped = jnp.dot(jnp.dot(left_root, grad_block, precision=HIGHEST), right_root, precision=HIGHEST) * col_mask
    graft_scale = jnp.sqrt(jnp.sum(adam_dir * adam_dir) + EPS_NORM) / jnp.sqrt(jnp.sum(shaped * shaped) + EPS_NORM)
    moment_new = BETA_MOMENT * moment + graft_scale * shaped
    return (left_new, right_new, moment_new, second_new)

def pick_rows(table_row, source):
    return jnp.take(source, table_row, axis=0)

def reference(grads, owner_table, momentum, second, left_stat, right_stat, left_root, right_root):
    summed = grads[0].astype(jnp.float32)
    for replica_id in range(1, N_REPLICA):
        summed = summed + grads[replica_id].astype(jnp.float32)
    padded = summed.reshape(RB, BLOCK, N_REPLICA, QW)
    padded = jnp.pad(padded, ((0, 0), (0, 0), (0, 0), (0, CBQ * BLOCK - QW)))
    blocks = padded.reshape(RB, BLOCK, N_REPLICA, CBQ, BLOCK).transpose(2, 0, 3, 1, 4).reshape(N_REPLICA, NB, BLOCK, BLOCK)
    owner_ids = jnp.arange(N_SHARD, dtype=jnp.int32)
    block_ids = jnp.arange(NB, dtype=jnp.int32)
    matches = owner_table[:, None, :] == owner_ids[None, :, None]
    inverse = lax.optimization_barrier(jnp.sum(jnp.where(matches, block_ids[None, None, :], 0), axis=2)).astype(jnp.int32)

    def group_step(group_id):

        def owner_step(owner_id):
            block_id = inverse[group_id, owner_id]
            grad_block = blocks[group_id, block_id]
            columns = block_id % CBQ * BLOCK + jnp.arange(BLOCK, dtype=jnp.int32)
            col_mask = (columns < QW).astype(jnp.float32)[None, :]
            return owner_update(grad_block, col_mask, left_stat[group_id, owner_id], right_stat[group_id, owner_id], left_root[group_id, owner_id], right_root[group_id, owner_id], momentum[group_id, owner_id], second[group_id, owner_id])
        return lax.map(owner_step, owner_ids)
    left_out, right_out, momentum_out, second_out = lax.map(group_step, jnp.arange(N_REPLICA, dtype=jnp.int32))
    step_blocks = (-LEARN_RATE * momentum_out).astype(jnp.bfloat16)
    by_block = jax.vmap(pick_rows)(owner_table, step_blocks)
    placed = by_block.reshape(N_REPLICA, RB, CBQ, BLOCK, BLOCK).transpose(1, 3, 0, 2, 4).reshape(RB, BLOCK, N_REPLICA, CBQ * BLOCK)
    update = placed[:, :, :, :QW].reshape(RB, BLOCK, D)
    return (update, momentum_out, second_out, left_out, right_out)
```

```python
import functools

import jax
import jax.numpy as jnp
from jax import lax
from jax.experimental import pallas as pl
from jax.experimental.pallas import tpu as pltpu
from jax.sharding import PartitionSpec as P

BETA_STAT = 0.95
BETA_SECOND = 0.99
BETA_MOMENT = 0.9
EPS_ADAM = 1e-08
EPS_NORM = 1e-06
LEARN_RATE = 0.5
MESH = pl.DeviceIdType.MESH
F32 = jnp.float32
BF16 = jnp.bfloat16
CHUNKS = 2


def kernel(cfg, inv_ref, tab_ref, g_ref, mom_in, sec_in, ls_in, rs_in, lr_in, rr_in, upd_out, mom_out, sec_out, left_out, right_out, *scratch):
    groups, shards, rb, rows_dev, quarter, block, n, width = cfg
    half = rb // 2
    scratch = list(scratch)

    def take(count):
        got = scratch[:count]
        del scratch[:count]
        return got

    own_p, from_next, from_prev = take(n), take(n), take(n)
    relay = [take(2) for _ in range(n)]
    relay_own = [take(2) for _ in range(n)]
    out_p, arrived = take(n), take(n)
    mom, sec, ls, rs, lr, rr = take(6)
    lroot, rroot, gb, shaped, back, back_arrived, upd = take(7)
    in_sem, own_sem, relay_own_sem, y_send, y_recv, a_send, a_recv, b_send, b_recv, o_sem = take(10)

    r, s = lax.axis_index("replica"), lax.axis_index("shard")
    nxt, prv, opp = lax.rem(r + 1, groups), lax.rem(r + groups - 1, groups), lax.rem(r + 2, groups)

    barrier = pltpu.get_barrier_semaphore()
    for peer in (nxt, prv):
        pl.semaphore_signal(barrier, inc=1, device_id=(peer, s), device_id_type=MESH)

    def greet(k, carry):
        pl.semaphore_signal(barrier, inc=1, device_id=(r, lax.rem(s + k, shards)), device_id_type=MESH)
        return carry

    lax.fori_loop(1, shards, greet, 0)

    def part(j, c):
        start = c * block + j * width
        return start, min(width, quarter - start)

    def piece(q, lo, rows, j, c):
        start, wide = part(j, c)
        return g_ref.at[pl.ds(lo, rows), :, pl.ds(pl.multiple_of(q * quarter + start, 128), wide)]

    parts = [(j, c) for j in range(n) for c in range(2)]
    own_copies = {}
    for j, c in parts:
        wide = part(j, c)[1]
        own_copies[j, c] = [
            pltpu.make_async_copy(piece(prv, 0, half, j, c), relay_own[j][0].at[c, :, :, pl.ds(0, wide)], relay_own_sem.at[j, 0, c]),
            pltpu.make_async_copy(piece(nxt, half, half, j, c), relay_own[j][1].at[c, :, :, pl.ds(0, wide)], relay_own_sem.at[j, 1, c]),
            pltpu.make_async_copy(piece(r, 0, rb, j, c), own_p[j].at[c, :, :, pl.ds(0, wide)], own_sem.at[j, c]),
        ]
        for copy in own_copies[j, c]:
            copy.start()
        if wide < width:
            for buf in (own_p[j], from_next[j], from_prev[j]):
                buf[c, :, :, wide:] = jnp.zeros((rb, rows_dev, width - wide), BF16)
    in_copies = [
        pltpu.make_async_copy(src, dst, in_sem.at[i])
        for i, (src, dst) in enumerate(((lr_in, lr), (rr_in, rr), (sec_in, sec), (mom_in, mom), (ls_in, ls), (rs_in, rs)))
    ]
    for copy in in_copies:
        copy.start()

    def y_copy(kind, way, j, c, src, dst):
        return pltpu.make_async_remote_copy(
            src_ref=src,
            dst_ref=dst,
            send_sem=y_send.at[kind, way, j, c],
            recv_sem=y_recv.at[kind, way, j, c],
            device_id=(nxt if way else prv, s),
            device_id_type=MESH,
        )

    first, direct, onward = {}, {}, {}
    for j, c in parts:
        wide = pl.ds(0, part(j, c)[1])
        lower, upper = pl.ds(0, half), pl.ds(half, half)
        first[j, c] = [
            y_copy(0, 0, j, c, piece(opp, 0, half, j, c), relay[j][0].at[c, :, :, wide]),
            y_copy(0, 1, j, c, piece(opp, half, half, j, c), relay[j][1].at[c, :, :, wide]),
        ]
        direct[j, c] = [
            y_copy(1, 0, j, c, piece(prv, half, half, j, c), from_next[j].at[c, upper, :, wide]),
            y_copy(1, 1, j, c, piece(nxt, 0, half, j, c), from_prev[j].at[c, lower, :, wide]),
        ]
        onward[j, c] = [
            y_copy(2, 0, j, c, relay[j][0].at[c, :, :, wide], from_next[j].at[c, lower, :, wide]),
            y_copy(2, 1, j, c, relay[j][1].at[c, :, :, wide], from_prev[j].at[c, upper, :, wide]),
        ]

    def start(table, j):
        if j < n:
            for c in range(2):
                for copy in table[j, c]:
                    copy.start()

    pl.semaphore_wait(barrier, shards - 1 + 2)
    start(first, 0)
    start(direct, 0)
    start(first, 1)

    for copy in in_copies[:2]:
        copy.wait()
    tile = 128

    def cast_roots(t, carry):
        at = pl.ds(pl.multiple_of(t * tile, tile), tile)
        lroot[at, :] = lr[at, :].astype(BF16)
        rroot[at, :] = rr[at, :].astype(BF16)
        return carry

    lax.fori_loop(0, block // tile, cast_roots, 0)

    def pass_on(j):
        for c in range(2):
            wide = part(j, c)[1]
            for way in range(2):
                own_copies[j, c][way].wait()
                first[j, c][way].wait_recv()
                buf, mine = relay[j][way], relay_own[j][way]
                both = buf[c, :, :, 0:wide].astype(F32) + mine[c, :, :, 0:wide].astype(F32)
                buf[c, :, :, 0:wide] = both.astype(BF16)
                onward[j, c][way].start()

    def hand_out(j):
        for c in range(2):
            own_copies[j, c][2].wait()
            for way in range(2):
                direct[j, c][way].wait_recv()
                onward[j, c][way].wait_recv()

        def total(d):
            b = inv_ref[d]
            c, i = lax.rem(b, 2), lax.div(b, 2)
            summed = own_p[j][c, i].astype(F32) + from_next[j][c, i].astype(F32) + from_prev[j][c, i].astype(F32)
            return summed.astype(BF16)

        def send(k, carry):
            d = lax.rem(s + k, shards)
            out_p[j][d] = total(d)
            pltpu.make_async_remote_copy(
                src_ref=out_p[j].at[d],
                dst_ref=arrived[j].at[s],
                send_sem=a_send.at[j],
                recv_sem=a_recv.at[j],
                device_id=(r, d),
                device_id_type=MESH,
            ).start()
            return carry

        lax.fori_loop(1, shards, send, 0)
        arrived[j][s] = total(s)

    def others(src, dst, sem):
        return pltpu.make_async_copy(src.at[pl.ds(0, shards - 1)], dst.at[pl.ds(0, shards - 1)], sem)

    for j in range(n):
        pass_on(j)
        start(direct, j + 1)
        start(first, j + 2)
        if j:
            hand_out(j - 1)
    hand_out(n - 1)

    for copy in in_copies[2:]:
        copy.wait()
    own_c = lax.rem(inv_ref[s], 2)
    real = quarter - own_c * block
    chunk_rows = 64
    adam_sq = jnp.zeros((8, width), F32)
    shaped_sq = jnp.zeros((8, block), F32)
    for j in range(n):
        others(out_p[j], arrived[j], a_recv.at[j]).wait()
        cols = slice(j * width, (j + 1) * width)

        def second_step(t, acc):
            at = pl.ds(pl.multiple_of(t * chunk_rows, chunk_rows), chunk_rows)
            g = arrived[j][pl.ds(pl.multiple_of(t * (chunk_rows // 8), 8), chunk_rows // 8)].astype(F32).reshape(chunk_rows, width)
            gb[at, cols] = g.astype(BF16)
            second = BETA_SECOND * sec[at, cols] + (1.0 - BETA_SECOND) * g * g
            sec[at, cols] = second
            adam = g / (jnp.sqrt(second) + EPS_ADAM)
            return acc + jnp.sum((adam * adam).reshape(chunk_rows // 8, 8, width), axis=0)

        adam_sq = lax.fori_loop(0, block // chunk_rows, second_step, adam_sq)

        def shape_step(t, acc):
            at = pl.ds(pl.multiple_of(t * tile, tile), tile)
            left = jnp.dot(lroot[at, :], gb[:, cols], preferred_element_type=F32).astype(BF16)
            both = jnp.dot(left, rroot[cols, :], preferred_element_type=F32)
            if j:
                both = both + shaped[at, :]
            if j == n - 1:
                both = jnp.where(lax.broadcasted_iota(jnp.int32, (tile, block), 1) < real, both, 0.0)
                acc = acc + jnp.sum((both * both).reshape(tile // 8, 8, block), axis=0)
            shaped[at, :] = both
            return acc

        shaped_sq = lax.fori_loop(0, block // tile, shape_step, shaped_sq)

    adam_norm = jnp.sum(jnp.sum(adam_sq, axis=0, keepdims=True), axis=1, keepdims=True)
    shaped_norm = jnp.sum(jnp.sum(shaped_sq, axis=0, keepdims=True), axis=1, keepdims=True)
    scale = jnp.sqrt(adam_norm + EPS_NORM) / jnp.sqrt(shaped_norm + EPS_NORM)

    per = chunk_rows // 8
    turns = shards // per

    def moment_step(k, carry):
        t = lax.rem(lax.div(s, per) + k, turns)
        at = pl.ds(pl.multiple_of(t * chunk_rows, chunk_rows), chunk_rows)
        moment = BETA_MOMENT * mom[at, :] + scale * shaped[at, :]
        mom[at, :] = moment
        back[pl.ds(pl.multiple_of(t * per, per), per)] = (-LEARN_RATE * moment).reshape(per, 8, block).astype(BF16)
        for i in range(per):
            d = t * per + i

            @pl.when(d != s)
            def _():
                pltpu.make_async_remote_copy(
                    src_ref=back.at[d],
                    dst_ref=back_arrived.at[s],
                    send_sem=b_send,
                    recv_sem=b_recv,
                    device_id=(r, d),
                    device_id_type=MESH,
                ).start()

        return carry

    lax.fori_loop(0, turns, moment_step, 0)
    back_arrived[s] = back[s]

    out_copies = [
        pltpu.make_async_copy(src, dst, o_sem.at[i])
        for i, (src, dst) in enumerate(((mom, mom_out), (sec, sec_out), (ls, left_out), (rs, right_out)))
    ]
    out_copies[0].start()
    out_copies[1].start()

    def left_step(t, carry):
        at = pl.ds(pl.multiple_of(t * tile, tile), tile)
        gram = lax.dot_general(gb[at, :], gb[...], (((1,), (1,)), ((), ())), preferred_element_type=F32)
        ls[at, :] = BETA_STAT * ls[at, :] + (1.0 - BETA_STAT) * gram
        return carry

    lax.fori_loop(0, block // tile, left_step, 0)
    out_copies[2].start()

    for t in range(block // tile):
        at = slice(t * tile, (t + 1) * tile)
        gram = lax.dot_general(gb[:, at], gb[...], (((0,), (0,)), ((), ())), preferred_element_type=F32)
        rs[at, :] = BETA_STAT * rs[at, :] + (1.0 - BETA_STAT) * gram
    out_copies[3].start()

    others(back, back_arrived, b_recv).wait()

    def place(i, carry):
        upd[i, :, 0:block] = back_arrived[tab_ref[2 * i]]
        upd[i, :, block:quarter] = back_arrived[tab_ref[2 * i + 1]][:, 0 : quarter - block]
        return carry

    lax.fori_loop(0, rb, place, 0)
    last = pltpu.make_async_copy(upd, upd_out, o_sem.at[4])
    last.start()
    for table in (first, direct, onward):
        for pair in table.values():
            for copy in pair:
                copy.wait_send()
    for j in range(n):
        others(out_p[j], arrived[j], a_send.at[j]).wait()
    others(back, back_arrived, b_send).wait()
    for copy in out_copies:
        copy.wait()
    last.wait()


def per_device(grads, owner_table, momentum, second, left_stat, right_stat, left_root, right_root):
    groups, shards = lax.axis_size("replica"), lax.axis_size("shard")
    _, rb, rows_dev, full_width = grads.shape
    block = left_stat.shape[2]
    quarter = full_width // groups
    n = CHUNKS
    width = block // n
    replica_index = lax.axis_index("replica")
    own_table = lax.dynamic_index_in_dim(owner_table, replica_index, 0, keepdims=False)
    ids = jnp.arange(shards, dtype=jnp.int32)
    inverse = jnp.sum(jnp.where(own_table[None, :] == ids[:, None], ids[None, :], 0), axis=1)
    cfg = (groups, shards, rb, rows_dev, quarter, block, n, width)
    sq = (block, block)
    whole = pltpu.VMEM((2, rb, rows_dev, width), BF16)
    halves = pltpu.VMEM((2, rb // 2, rows_dev, width), BF16)
    slots = pltpu.VMEM((shards, rows_dev, width), BF16)
    wide_slots = pltpu.VMEM((shards, rows_dev, block), BF16)
    dma = pltpu.SemaphoreType.DMA
    any_spec = pl.BlockSpec(memory_space=pl.ANY)
    smem = pl.BlockSpec(memory_space=pltpu.SMEM)
    update, moment_new, second_new, left_new, right_new = pl.pallas_call(
        functools.partial(kernel, cfg),
        name="shampoo_step",
        out_shape=(jax.ShapeDtypeStruct((rb, rows_dev, quarter), BF16),) + (jax.ShapeDtypeStruct(sq, F32),) * 4,
        in_specs=[smem, smem] + [any_spec] * 7,
        out_specs=[any_spec] * 5,
        scratch_shapes=[whole] * (3 * n)
        + [halves] * (4 * n)
        + [slots] * (2 * n)
        + [pltpu.VMEM(sq, F32)] * 6
        + [pltpu.VMEM(sq, BF16)] * 3
        + [pltpu.VMEM(sq, F32), wide_slots, wide_slots, pltpu.VMEM((rb, rows_dev, quarter), BF16)]
        + [dma((6,)), dma((n, 2)), dma((n, 2, 2)), dma((3, 2, n, 2)), dma((3, 2, n, 2)), dma((n,)), dma((n,)), dma, dma, dma((5,))],
        compiler_params=pltpu.CompilerParams(collective_id=1, has_side_effects=True, vmem_limit_bytes=60 * 2**20),
        cost_estimate=pl.CostEstimate(flops=8 * block**3, bytes_accessed=16 * 2**20, transcendentals=0),
    )(inverse, own_table, grads[0], momentum[0, 0], second[0, 0], left_stat[0, 0], right_stat[0, 0], left_root[0, 0], right_root[0, 0])
    shape_own = (1, 1, block, block)
    return (
        update,
        moment_new.reshape(shape_own),
        second_new.reshape(shape_own),
        left_new.reshape(shape_own),
        right_new.reshape(shape_own),
    )


def solution(mesh):
    owned = P("replica", "shard", None, None)
    return jax.shard_map(
        per_device,
        mesh=mesh,
        in_specs=(P("replica", None, "shard", None), P(), owned, owned, owned, owned, owned, owned),
        out_specs=(P(None, "shard", "replica"), owned, owned, owned, owned),
        check_vma=False,
    )
```

```python
import functools

import jax
import jax.numpy as jnp
from jax import lax
from jax.experimental import pallas as pl
from jax.experimental.pallas import tpu as pltpu
from jax.sharding import PartitionSpec as P

BETA_STAT = 0.95
BETA_SECOND = 0.99
BETA_MOMENT = 0.9
EPS_ADAM = 1e-08
EPS_NORM = 1e-06
LEARN_RATE = 0.5
MESH = pl.DeviceIdType.MESH
F32 = jnp.float32
BF16 = jnp.bfloat16
CHUNKS = 4
SPOTS = 8
SPLIT = 4


def kernel(cfg, table_in, g_in, mom_in, sec_in, ls_in, rs_in, lr_in, rr_in, back_arrived, mom, sec, ls, rs, *scratch):
    groups, shards, rb, rows_dev, quarter, block, n, width = cfg
    half = rb // 2
    scratch = list(scratch)

    def take(count):
        got = scratch[:count]
        del scratch[:count]
        return got

    from_next, from_prev, total = take(n), take(n), take(n)
    relay = [take(2) for _ in range(n)]
    out_p, arrived = take(n), take(n)
    lr, rr, lroot, rroot, gb, shaped, back, g_ref, table_ref, inv_v, inv_ref = take(11)
    in_sem, g_sem, inv_sem, y_send, y_recv, a_send, a_recv, b_send, b_recv, near_in, line_in, all_in = take(12)

    r, s = lax.axis_index("replica"), lax.axis_index("shard")
    nxt, prv, opp = lax.rem(r + 1, groups), lax.rem(r + groups - 1, groups), lax.rem(r + 2, groups)

    barrier = pltpu.get_barrier_semaphore()
    plane, spot, planes = lax.div(s, SPOTS), lax.rem(s, SPOTS), shards // SPOTS
    in_plane = [(r, plane * SPOTS + lax.rem(spot + k, SPOTS)) for k in range(1, SPOTS)]
    in_line = [(r, lax.rem(plane + k, planes) * SPOTS + spot) for k in range(planes)]
    near = [(nxt, s), (prv, s), in_line[1], in_line[planes - 1]] + in_plane
    for peer in near:
        pl.semaphore_signal(barrier, inc=1, device_id=peer, device_id_type=MESH)

    def columns(q):
        return pl.ds(pl.multiple_of(q * quarter, 128), quarter)

    g_copies = [
        pltpu.make_async_copy(g_in.at[:, :, columns(q)], g_ref.at[:, :, columns(q)], g_sem.at[i])
        for i, q in enumerate((opp, nxt, prv, r))
    ]
    for copy in g_copies:
        copy.start()

    table_copy = pltpu.make_async_copy(table_in, table_ref, inv_sem.at[0])
    table_copy.start()

    table_copy.wait()
    table = table_ref[pl.ds(r, 1), :]
    rows = lax.broadcasted_iota(jnp.int32, (shards, shards), 0)
    cols = lax.broadcasted_iota(jnp.int32, (shards, shards), 1)
    column = jnp.sum(jnp.where(rows == cols, table, 0), axis=1, keepdims=True)
    inv_v[...] = jnp.zeros_like(inv_v)
    inv_v[:, 0:shards] = jnp.max(jnp.where(column == cols, rows, 0), axis=0, keepdims=True)
    inv_copy = pltpu.make_async_copy(inv_v, inv_ref, inv_sem.at[1])
    inv_copy.start()

    def part(j, c):
        start = c * block + j * width
        return start, max(0, min(width, quarter - start))

    def piece(q, lo, rows, j, c):
        start, wide = part(j, c)
        return g_ref.at[pl.ds(lo, rows), :, pl.ds(pl.multiple_of(q * quarter + start, 128), wide)]

    parts = [(j, c) for j in range(n) for c in range(2) if part(j, c)[1] > 0]
    for j in range(n):
        wide = part(j, 1)[1]
        if wide < width:
            total[j][1, :, :, wide:] = jnp.zeros((rb, rows_dev, width - wide), BF16)
    def y_copy(kind, way, j, c, src, dst):
        return pltpu.make_async_remote_copy(
            src_ref=src,
            dst_ref=dst,
            send_sem=y_send.at[kind, way, j, c],
            recv_sem=y_recv.at[kind, way, j, c],
            device_id=(nxt if way else prv, s),
            device_id_type=MESH,
        )

    first, direct, onward = {}, {}, {}
    for j, c in parts:
        wide = pl.ds(0, part(j, c)[1])
        lower, upper = pl.ds(0, half), pl.ds(half, half)
        first[j, c] = [
            y_copy(0, 0, j, c, piece(opp, 0, half, j, c), relay[j][0].at[c, :, :, wide]),
            y_copy(0, 1, j, c, piece(opp, half, half, j, c), relay[j][1].at[c, :, :, wide]),
        ]
        direct[j, c] = [
            y_copy(1, 0, j, c, piece(prv, half, half, j, c), from_next[j].at[c, upper, :, wide]),
            y_copy(1, 1, j, c, piece(nxt, 0, half, j, c), from_prev[j].at[c, lower, :, wide]),
        ]
        onward[j, c] = [
            y_copy(2, 0, j, c, relay[j][0].at[c, :, :, wide], from_next[j].at[c, lower, :, wide]),
            y_copy(2, 1, j, c, relay[j][1].at[c, :, :, wide], from_prev[j].at[c, upper, :, wide]),
        ]

    def start(table, j):
        if j < n:
            for c in range(2):
                for copy in table.get((j, c), ()):
                    copy.start()

    g_copies[0].wait()
    def tell(peers, sem):
        for peer in peers:
            pl.semaphore_signal(sem, inc=1, device_id=peer, device_id_type=MESH)

    pl.semaphore_wait(barrier, len(near))
    tell((in_line[1], in_line[planes - 1]), near_in)
    for j in range(n):
        start(first, j)
    for copy in g_copies[1:]:
        copy.wait()
    start(direct, 0)
    pl.semaphore_wait(near_in, 2)
    tell((in_line[2], in_line[planes - 2]), line_in)

    in_copies = [
        pltpu.make_async_copy(src, dst, in_sem.at[i])
        for i, (src, dst) in enumerate(((lr_in, lr), (rr_in, rr), (sec_in, sec), (mom_in, mom), (ls_in, ls), (rs_in, rs)))
    ]
    for copy in in_copies:
        copy.start()

    tile = 128

    def mine(q, lo, count, j, c):
        start, wide = part(j, c)
        return g_ref[pl.ds(lo, count), :, pl.ds(pl.multiple_of(q * quarter + start, 128), wide)].astype(F32)

    def pass_on(j):
        for c in range(2):
            wide = part(j, c)[1]
            for way, q, lo in ((0, prv, 0), (1, nxt, half)) if wide else ():
                first[j, c][way].wait_recv()
                buf = relay[j][way]
                buf[c, :, :, 0:wide] = (buf[c, :, :, 0:wide].astype(F32) + mine(q, lo, half, j, c)).astype(BF16)
                onward[j, c][way].start()

    def hand_out(j):
        for c in range(2):
            wide = part(j, c)[1]
            if not wide:
                continue
            for way in range(2):
                direct[j, c][way].wait_recv()
                onward[j, c][way].wait_recv()
            summed = mine(r, 0, rb, j, c) + from_next[j][c, :, :, 0:wide].astype(F32) + from_prev[j][c, :, :, 0:wide].astype(F32)
            total[j][c, :, :, 0:wide] = summed.astype(BF16)

        def block_of(d):
            b = inv_ref[0, d]
            return total[j][lax.rem(b, 2), lax.div(b, 2)]

        def send(k, carry):
            d = lax.rem(s + k, shards)
            out_p[j][d] = block_of(d)
            pltpu.make_async_remote_copy(
                src_ref=out_p[j].at[d],
                dst_ref=arrived[j].at[s],
                send_sem=a_send.at[j],
                recv_sem=a_recv.at[j],
                device_id=(r, d),
                device_id_type=MESH,
            ).start()
            return carry

        lax.fori_loop(1, shards, send, 0, unroll=9)
        arrived[j][s] = block_of(s)

    def others(src, dst, sem):
        return pltpu.make_async_copy(src.at[pl.ds(0, shards - 1)], dst.at[pl.ds(0, shards - 1)], sem)

    inv_copy.wait()
    for j in range(n):
        pass_on(j)
        start(direct, j + 1)
        if j == 0:
            pl.semaphore_wait(line_in, 2)
            tell(in_plane, all_in)
    pl.semaphore_wait(all_in, len(in_plane))
    for j in range(n):
        hand_out(j)

    for copy in in_copies[:2]:
        copy.wait()

    def cast_roots(t, carry):
        at = pl.ds(pl.multiple_of(t * tile, tile), tile)
        lroot[at, :] = lr[at, :].astype(BF16)
        rroot[at, :] = rr[at, :].astype(BF16)
        return carry

    lax.fori_loop(0, block // tile, cast_roots, 0)

    for copy in in_copies[2:]:
        copy.wait()
    own_c = lax.rem(inv_ref[0, s], 2)
    real = quarter - own_c * block
    chunk_rows = 64
    adam_sq = jnp.zeros((8, width), F32)
    shaped_sq = jnp.zeros((8, block), F32)
    for j in range(n):
        others(out_p[j], arrived[j], a_recv.at[j]).wait()
        cols = slice(j * width, (j + 1) * width)

        def second_step(t, acc):
            at = pl.ds(pl.multiple_of(t * chunk_rows, chunk_rows), chunk_rows)
            g = arrived[j][pl.ds(pl.multiple_of(t * (chunk_rows // 8), 8), chunk_rows // 8)].astype(F32).reshape(chunk_rows, width)
            gb[at, cols] = g.astype(BF16)
            second = BETA_SECOND * sec[at, cols] + (1.0 - BETA_SECOND) * g * g
            sec[at, cols] = second
            adam = g / (jnp.sqrt(second) + EPS_ADAM)
            return acc + jnp.sum((adam * adam).reshape(chunk_rows // 8, 8, width), axis=0)

        adam_sq = lax.fori_loop(0, block // chunk_rows, second_step, adam_sq)

        def shape_step(t, acc):
            at = pl.ds(pl.multiple_of(t * tile, tile), tile)
            left = jnp.dot(lroot[at, :], gb[:, cols], preferred_element_type=F32).astype(BF16)
            both = jnp.dot(left, rroot[cols, :], preferred_element_type=F32)
            if j:
                both = both + shaped[at, :]
            if j == n - 1:
                both = jnp.where(lax.broadcasted_iota(jnp.int32, (tile, block), 1) < real, both, 0.0)
                acc = acc + jnp.sum((both * both).reshape(tile // 8, 8, block), axis=0)
            shaped[at, :] = both
            return acc

        shaped_sq = lax.fori_loop(0, block // tile, shape_step, shaped_sq)

    adam_norm = jnp.sum(jnp.sum(adam_sq, axis=0, keepdims=True), axis=1, keepdims=True)
    shaped_norm = jnp.sum(jnp.sum(shaped_sq, axis=0, keepdims=True), axis=1, keepdims=True)
    scale = jnp.sqrt(adam_norm + EPS_NORM) / jnp.sqrt(shaped_norm + EPS_NORM)

    per = chunk_rows // 8
    turns = shards // per

    def moment_step(k, carry):
        t = lax.rem(lax.div(s, per) + k, turns)
        at = pl.ds(pl.multiple_of(t * chunk_rows, chunk_rows), chunk_rows)
        moment = BETA_MOMENT * mom[at, :] + scale * shaped[at, :]
        mom[at, :] = moment
        back[pl.ds(pl.multiple_of(t * per, per), per)] = (-LEARN_RATE * moment).reshape(per, 8, block).astype(BF16)
        for i in range(per):
            d = t * per + i

            @pl.when(d != s)
            def _():
                pltpu.make_async_remote_copy(
                    src_ref=back.at[d],
                    dst_ref=back_arrived.at[s],
                    send_sem=b_send,
                    recv_sem=b_recv,
                    device_id=(r, d),
                    device_id_type=MESH,
                ).start()

        return carry

    lax.fori_loop(0, turns, moment_step, 0)
    back_arrived[s] = back[s]

    def left_step(t, carry):
        at = pl.ds(pl.multiple_of(t * tile, tile), tile)
        gram = lax.dot_general(gb[at, :], gb[...], (((1,), (1,)), ((), ())), preferred_element_type=F32)
        ls[at, :] = BETA_STAT * ls[at, :] + (1.0 - BETA_STAT) * gram
        return carry

    lax.fori_loop(0, block // tile, left_step, 0)

    for t in range(block // tile):
        at = slice(t * tile, (t + 1) * tile)
        gram = lax.dot_general(gb[:, at], gb[...], (((0,), (0,)), ((), ())), preferred_element_type=F32)
        rs[at, :] = BETA_STAT * rs[at, :] + (1.0 - BETA_STAT) * gram

    others(back, back_arrived, b_recv).wait()

    for table in (first, direct, onward):
        for pair in table.values():
            for copy in pair:
                copy.wait_send()
    for j in range(n):
        others(out_p[j], arrived[j], a_send.at[j]).wait()
    others(back, back_arrived, b_send).wait()


def finish(quarter, block, table_ref, arrived, mom, sec, ls, rs, upd_out, mom_out, sec_out, left_out, right_out, upd, sem):
    pairs = ((mom, mom_out), (sec, sec_out), (ls, left_out), (rs, right_out))
    rows = block // SPLIT
    copies = [
        pltpu.make_async_copy(src.at[pl.ds(k * rows, rows)], dst.at[pl.ds(k * rows, rows)], sem.at[i * SPLIT + k])
        for i, (src, dst) in enumerate(pairs)
        for k in range(SPLIT)
    ]
    for copy in copies:
        copy.start()

    r = lax.axis_index("replica")

    def place(i, carry):
        upd[i, :, 0:block] = arrived[table_ref[r, 2 * i]]
        upd[i, :, block:quarter] = arrived[table_ref[r, 2 * i + 1]][:, 0 : quarter - block]
        return carry

    lax.fori_loop(0, upd.shape[0], place, 0)
    last = pltpu.make_async_copy(upd, upd_out, sem.at[4 * SPLIT])
    last.start()
    for copy in copies:
        copy.wait()
    last.wait()


def per_device(grads, owner_table, momentum, second, left_stat, right_stat, left_root, right_root):
    groups, shards = lax.axis_size("replica"), lax.axis_size("shard")
    _, rb, rows_dev, full_width = grads.shape
    block = left_stat.shape[2]
    quarter = full_width // groups
    n = CHUNKS
    width = block // n
    cfg = (groups, shards, rb, rows_dev, quarter, block, n, width)
    sq = (block, block)
    whole = pltpu.VMEM((2, rb, rows_dev, width), BF16)
    halves = pltpu.VMEM((2, rb // 2, rows_dev, width), BF16)
    slots = pltpu.VMEM((shards, rows_dev, width), BF16)
    wide_slots = pltpu.VMEM((shards, rows_dev, block), BF16)
    dma = pltpu.SemaphoreType.DMA
    hbm = pl.BlockSpec(memory_space=pltpu.HBM)
    vmem = pl.BlockSpec(memory_space=pltpu.VMEM)
    smem = pl.BlockSpec(memory_space=pltpu.SMEM)
    operands = (owner_table, grads[0], *[a[0, 0] for a in (momentum, second, left_stat, right_stat, left_root, right_root)])
    results = pl.pallas_call(
        functools.partial(kernel, cfg),
        name="shampoo_step",
        out_shape=(pltpu.VMEM((shards, rows_dev, block), BF16),) + (pltpu.VMEM(sq, F32),) * 4,
        in_specs=[hbm] * 8,
        out_specs=[vmem] * 5,
        scratch_shapes=[whole] * (3 * n)
        + [halves] * (2 * n)
        + [slots] * (2 * n)
        + [pltpu.VMEM(sq, F32)] * 2
        + [pltpu.VMEM(sq, BF16)] * 3
        + [pltpu.VMEM(sq, F32), wide_slots, pltpu.VMEM((rb, rows_dev, full_width), BF16)]
        + [pltpu.VMEM(owner_table.shape, jnp.int32), pltpu.VMEM((1, 128), jnp.int32), pltpu.SMEM((1, 128), jnp.int32)]
        + [dma((6,)), dma((4,)), dma((2,)), dma((3, 2, n, 2)), dma((3, 2, n, 2)), dma((n,)), dma((n,)), dma, dma] + [pltpu.SemaphoreType.REGULAR] * 3,
        compiler_params=pltpu.CompilerParams(collective_id=1, has_side_effects=True, vmem_limit_bytes=40 * 2**20),
        cost_estimate=pl.CostEstimate(flops=8 * block**3, bytes_accessed=16 * 2**20, transcendentals=0),
    )(*[pltpu.with_memory_space_constraint(a, pltpu.HBM) for a in operands])
    update, moment_new, second_new, left_new, right_new = pl.pallas_call(
        functools.partial(finish, quarter, block),
        name="place_update",
        out_shape=(jax.ShapeDtypeStruct((rb, rows_dev, quarter), BF16),) + (jax.ShapeDtypeStruct(sq, F32),) * 4,
        in_specs=[smem] + [vmem] * 5,
        out_specs=[hbm] * 5,
        scratch_shapes=[pltpu.VMEM((rb, rows_dev, quarter), BF16), dma((4 * SPLIT + 1,))],
        compiler_params=pltpu.CompilerParams(vmem_limit_bytes=8 * 2**20),
    )(owner_table, *results)
    shape_own = (1, 1, block, block)
    return (
        update,
        moment_new.reshape(shape_own),
        second_new.reshape(shape_own),
        left_new.reshape(shape_own),
        right_new.reshape(shape_own),
    )


def solution(mesh):
    owned = P("replica", "shard", None, None)
    return jax.shard_map(
        per_device,
        mesh=mesh,
        in_specs=(P("replica", None, "shard", None), P(), owned, owned, owned, owned, owned, owned),
        out_specs=(P(None, "shard", "replica"), owned, owned, owned, owned),
        check_vma=False,
    )
```

```python
import functools

import jax
import jax.numpy as jnp
from jax import lax
from jax.experimental import pallas as pl
from jax.experimental.pallas import tpu as pltpu
from jax.sharding import PartitionSpec as P

BETA_STAT = 0.95
BETA_SECOND = 0.99
BETA_MOMENT = 0.9
EPS_ADAM = 1e-08
EPS_NORM = 1e-06
LEARN_RATE = 0.5
MESH = pl.DeviceIdType.MESH
F32 = jnp.float32
BF16 = jnp.bfloat16
CHUNKS = 4
SPOTS = 8
SPLIT = 1


def kernel(cfg, table_in, g_in, mom_in, sec_in, ls_in, rs_in, lr_in, rr_in, back_arrived, mom, sec, ls, rs, *scratch):
    groups, shards, rb, rows_dev, quarter, block, n, width = cfg
    half = rb // 2
    scratch = list(scratch)

    def take(count):
        got = scratch[:count]
        del scratch[:count]
        return got

    from_next, from_prev, total = take(n), take(n), take(n)
    relay = [take(2) for _ in range(n)]
    (from_opp,) = take(1)
    out_p, arrived = take(n), take(n)
    lr, rr, lroot, rroot, gb, shaped, back, g_ref, table_ref, inv_v, inv_ref = take(11)
    in_sem, g_sem, inv_sem, d_send, d_recv, y_send, y_recv, a_send, a_recv, b_send, b_recv, near_in, line_in, all_in = take(14)

    r, s = lax.axis_index("replica"), lax.axis_index("shard")
    nxt, prv, opp = lax.rem(r + 1, groups), lax.rem(r + groups - 1, groups), lax.rem(r + 2, groups)

    barrier = pltpu.get_barrier_semaphore()
    plane, spot, planes = lax.div(s, SPOTS), lax.rem(s, SPOTS), shards // SPOTS
    in_plane = [(r, plane * SPOTS + lax.rem(spot + k, SPOTS)) for k in range(1, SPOTS)]
    in_line = [(r, lax.rem(plane + k, planes) * SPOTS + spot) for k in range(planes)]
    near = [(nxt, s), (prv, s), (opp, s), in_line[1], in_line[planes - 1]] + in_plane
    def greet(peers):
        for peer in peers:
            pl.semaphore_signal(barrier, inc=1, device_id=peer, device_id_type=MESH)

    greet(near[:3])

    early, late = n - 1, list(range(n - 1))
    spans = [(early * width, width), (0, early * width), (block, quarter - block)]

    def load(i, q, k):
        lo, wide = spans[k]
        at = pl.ds(pl.multiple_of(q * quarter + lo, 128), wide)
        return pltpu.make_async_copy(g_in.at[:, :, at], g_ref.at[:, :, at], g_sem.at[i, k])

    loads = [[load(i, q, k) for k in range(3)] for i, q in enumerate((opp, nxt, prv, r))]
    for i in range(3):
        loads[i][0].start()
    greet(near[3:])
    for i in range(4):
        for k in range(1 if i < 3 else 0, 3):
            loads[i][k].start()
    table_copy = pltpu.make_async_copy(table_in, table_ref, inv_sem.at[0])
    table_copy.start()
    def part(j, c):
        start = c * block + j * width
        return start, max(0, min(width, quarter - start))

    def piece(q, lo, rows, j, c):
        start, wide = part(j, c)
        return g_ref.at[pl.ds(lo, rows), :, pl.ds(pl.multiple_of(q * quarter + start, 128), wide)]

    parts = [(j, c) for j in range(n) for c in range(2) if part(j, c)[1] > 0]
    for j in range(n):
        wide = part(j, 1)[1]
        if wide < width:
            total[j][1, :, :, wide:] = jnp.zeros((rb, rows_dev, width - wide), BF16)
    def y_copy(kind, way, j, c, src, dst):
        return pltpu.make_async_remote_copy(
            src_ref=src,
            dst_ref=dst,
            send_sem=y_send.at[kind, way, j, c],
            recv_sem=y_recv.at[kind, way, j, c],
            device_id=(nxt if way else prv, s),
            device_id_type=MESH,
        )

    first, direct, onward = {}, {}, {}
    for j, c in parts:
        if j == n - 1:
            continue
        wide = pl.ds(0, part(j, c)[1])
        lower, upper = pl.ds(0, half), pl.ds(half, half)
        first[j, c] = [
            y_copy(0, 0, j, c, piece(opp, 0, half, j, c), relay[j][0].at[c, :, :, wide]),
            y_copy(0, 1, j, c, piece(opp, half, half, j, c), relay[j][1].at[c, :, :, wide]),
        ]
        direct[j, c] = [
            y_copy(1, 0, j, c, piece(prv, half, half, j, c), from_next[j].at[c, upper, :, wide]),
            y_copy(1, 1, j, c, piece(nxt, 0, half, j, c), from_prev[j].at[c, lower, :, wide]),
        ]
        onward[j, c] = [
            y_copy(2, 0, j, c, relay[j][0].at[c, :, :, wide], from_next[j].at[c, lower, :, wide]),
            y_copy(2, 1, j, c, relay[j][1].at[c, :, :, wide], from_prev[j].at[c, upper, :, wide]),
        ]

    straight = [
        pltpu.make_async_remote_copy(
            src_ref=piece(q, 0, rb, early, c),
            dst_ref=buf.at[c, :, :, pl.ds(0, part(early, c)[1])],
            send_sem=d_send.at[i, c],
            recv_sem=d_recv.at[i, c],
            device_id=(q, s),
            device_id_type=MESH,
        )
        for i, (q, buf) in enumerate(((opp, from_opp), (nxt, from_prev[early]), (prv, from_next[early])))
        for c in range(2)
        if part(early, c)[1]
    ]

    def start(table, j):
        if j < n:
            for c in range(2):
                for copy in table.get((j, c), ()):
                    copy.start()

    def tell(peers, sem):
        for peer in peers:
            pl.semaphore_signal(sem, inc=1, device_id=peer, device_id_type=MESH)

    for i in range(3):
        loads[i][0].wait()
    pl.semaphore_wait(barrier, len(near))
    tell((in_line[1], in_line[planes - 1]), near_in)
    for copy in straight:
        copy.start()
    for copy in loads[0][1:]:
        copy.wait()
    for j in late:
        start(first, j)
    for copy in loads[1][1:] + loads[2][1:]:
        copy.wait()
    start(direct, 0)
    for copy in loads[3]:
        copy.wait()
    table_copy.wait()
    table = table_ref[pl.ds(r, 1), :]
    rows = lax.broadcasted_iota(jnp.int32, (shards, shards), 0)
    cols = lax.broadcasted_iota(jnp.int32, (shards, shards), 1)
    column = jnp.sum(jnp.where(rows == cols, table, 0), axis=1, keepdims=True)
    inv_v[...] = jnp.zeros_like(inv_v)
    inv_v[:, 0:shards] = jnp.max(jnp.where(column == cols, rows, 0), axis=0, keepdims=True)
    inv_copy = pltpu.make_async_copy(inv_v, inv_ref, inv_sem.at[1])
    inv_copy.start()

    pl.semaphore_wait(near_in, 2)
    tell((in_line[2], in_line[planes - 2]), line_in)
    pl.semaphore_wait(line_in, 2)
    tell(in_plane, all_in)

    in_copies = [
        pltpu.make_async_copy(src, dst, in_sem.at[i])
        for i, (src, dst) in enumerate(((lr_in, lr), (rr_in, rr), (sec_in, sec), (mom_in, mom), (ls_in, ls), (rs_in, rs)))
    ]
    for copy in in_copies:
        copy.start()

    tile = 128

    def mine(q, lo, count, j, c):
        start, wide = part(j, c)
        return g_ref[pl.ds(lo, count), :, pl.ds(pl.multiple_of(q * quarter + start, 128), wide)].astype(F32)

    def pass_on(j):
        for c in range(2):
            wide = part(j, c)[1]
            for way, q, lo in ((0, prv, 0), (1, nxt, half)) if wide else ():
                first[j, c][way].wait_recv()
                buf = relay[j][way]
                buf[c, :, :, 0:wide] = (buf[c, :, :, 0:wide].astype(F32) + mine(q, lo, half, j, c)).astype(BF16)
                onward[j, c][way].start()

    def hand_out(j):
        if j == early:
            for copy in straight:
                copy.wait_recv()
        for c in range(2):
            wide = part(j, c)[1]
            if not wide:
                continue
            if j != early:
                for way in range(2):
                    direct[j, c][way].wait_recv()
                    onward[j, c][way].wait_recv()
            summed = mine(r, 0, rb, j, c) + from_next[j][c, :, :, 0:wide].astype(F32) + from_prev[j][c, :, :, 0:wide].astype(F32)
            if j == early:
                summed = summed + from_opp[c, :, :, 0:wide].astype(F32)
            total[j][c, :, :, 0:wide] = summed.astype(BF16)

        def block_of(d):
            b = inv_ref[0, d]
            return total[j][lax.rem(b, 2), lax.div(b, 2)]

        def send(k, carry):
            d = lax.rem(s + k, shards)
            out_p[j][d] = block_of(d)
            pltpu.make_async_remote_copy(
                src_ref=out_p[j].at[d],
                dst_ref=arrived[j].at[s],
                send_sem=a_send.at[j],
                recv_sem=a_recv.at[j],
                device_id=(r, d),
                device_id_type=MESH,
            ).start()
            return carry

        lax.fori_loop(1, shards, send, 0, unroll=9)
        arrived[j][s] = block_of(s)

    def others(src, dst, sem):
        return pltpu.make_async_copy(src.at[pl.ds(0, shards - 1)], dst.at[pl.ds(0, shards - 1)], sem)

    inv_copy.wait()
    for j in late:
        pass_on(j)
        start(direct, j + 1)
        if j == min(1, late[-1]):
            pl.semaphore_wait(all_in, len(in_plane))
            hand_out(early)
    for j in late:
        hand_out(j)

    for copy in in_copies[:2]:
        copy.wait()

    def cast_roots(t, carry):
        at = pl.ds(pl.multiple_of(t * tile, tile), tile)
        lroot[at, :] = lr[at, :].astype(BF16)
        rroot[at, :] = rr[at, :].astype(BF16)
        return carry

    lax.fori_loop(0, block // tile, cast_roots, 0)

    for copy in in_copies[2:]:
        copy.wait()
    own_c = lax.rem(inv_ref[0, s], 2)
    real = quarter - own_c * block
    chunk_rows = 64
    adam_sq = jnp.zeros((8, width), F32)
    shaped_sq = jnp.zeros((8, block), F32)
    for j in [early] + late:
        others(out_p[j], arrived[j], a_recv.at[j]).wait()
        cols = slice(j * width, (j + 1) * width)

        def second_step(t, acc):
            at = pl.ds(pl.multiple_of(t * chunk_rows, chunk_rows), chunk_rows)
            g = arrived[j][pl.ds(pl.multiple_of(t * (chunk_rows // 8), 8), chunk_rows // 8)].astype(F32).reshape(chunk_rows, width)
            gb[at, cols] = g.astype(BF16)
            second = BETA_SECOND * sec[at, cols] + (1.0 - BETA_SECOND) * g * g
            sec[at, cols] = second
            adam = g / (jnp.sqrt(second) + EPS_ADAM)
            return acc + jnp.sum((adam * adam).reshape(chunk_rows // 8, 8, width), axis=0)

        adam_sq = lax.fori_loop(0, block // chunk_rows, second_step, adam_sq, unroll=True)

        def shape_step(t, acc):
            at = pl.ds(pl.multiple_of(t * tile, tile), tile)
            left = jnp.dot(lroot[at, :], gb[:, cols], preferred_element_type=F32).astype(BF16)
            both = jnp.dot(left, rroot[cols, :], preferred_element_type=F32)
            if j != early:
                both = both + shaped[at, :]
            if j == late[-1]:
                both = jnp.where(lax.broadcasted_iota(jnp.int32, (tile, block), 1) < real, both, 0.0)
                acc = acc + jnp.sum((both * both).reshape(tile // 8, 8, block), axis=0)
            shaped[at, :] = both
            return acc

        shaped_sq = lax.fori_loop(0, block // tile, shape_step, shaped_sq, unroll=True)

    adam_norm = jnp.sum(jnp.sum(adam_sq, axis=0, keepdims=True), axis=1, keepdims=True)
    shaped_norm = jnp.sum(jnp.sum(shaped_sq, axis=0, keepdims=True), axis=1, keepdims=True)
    scale = jnp.sqrt(adam_norm + EPS_NORM) / jnp.sqrt(shaped_norm + EPS_NORM)

    per = chunk_rows // 8
    turns = shards // per

    def moment_step(k, carry):
        t = lax.rem(lax.div(s, per) + k, turns)
        at = pl.ds(pl.multiple_of(t * chunk_rows, chunk_rows), chunk_rows)
        moment = BETA_MOMENT * mom[at, :] + scale * shaped[at, :]
        mom[at, :] = moment
        back[pl.ds(pl.multiple_of(t * per, per), per)] = (-LEARN_RATE * moment).reshape(per, 8, block).astype(BF16)
        for i in range(per):
            d = t * per + i

            @pl.when(d != s)
            def _():
                pltpu.make_async_remote_copy(
                    src_ref=back.at[d],
                    dst_ref=back_arrived.at[s],
                    send_sem=b_send,
                    recv_sem=b_recv,
                    device_id=(r, d),
                    device_id_type=MESH,
                ).start()

        return carry

    lax.fori_loop(0, turns, moment_step, 0)
    back_arrived[s] = back[s]

    def left_step(t, carry):
        at = pl.ds(pl.multiple_of(t * tile, tile), tile)
        gram = lax.dot_general(gb[at, :], gb[...], (((1,), (1,)), ((), ())), preferred_element_type=F32)
        ls[at, :] = BETA_STAT * ls[at, :] + (1.0 - BETA_STAT) * gram
        return carry

    lax.fori_loop(0, block // tile, left_step, 0)

    for t in range(block // tile):
        at = slice(t * tile, (t + 1) * tile)
        gram = lax.dot_general(gb[:, at], gb[...], (((0,), (0,)), ((), ())), preferred_element_type=F32)
        rs[at, :] = BETA_STAT * rs[at, :] + (1.0 - BETA_STAT) * gram

    others(back, back_arrived, b_recv).wait()

    for copy in straight:
        copy.wait_send()
    for table in (first, direct, onward):
        for pair in table.values():
            for copy in pair:
                copy.wait_send()
    for j in range(n):
        others(out_p[j], arrived[j], a_send.at[j]).wait()
    others(back, back_arrived, b_send).wait()


def finish(quarter, block, table_in, arrived, mom, sec, ls, rs, upd_out, mom_out, sec_out, left_out, right_out, upd, table_ref, sem, table_sem):
    table_copy = pltpu.make_async_copy(table_in, table_ref, table_sem)
    table_copy.start()
    pairs = ((mom, mom_out), (sec, sec_out), (ls, left_out), (rs, right_out))
    rows = block // SPLIT
    copies = [
        pltpu.make_async_copy(src.at[pl.ds(k * rows, rows)], dst.at[pl.ds(k * rows, rows)], sem.at[i * SPLIT + k])
        for i, (src, dst) in enumerate(pairs)
        for k in range(SPLIT)
    ]
    for copy in copies:
        copy.start()

    r = lax.axis_index("replica")
    table_copy.wait()

    def place(i, carry):
        upd[i, :, 0:block] = arrived[table_ref[r, 2 * i]]
        upd[i, :, block:quarter] = arrived[table_ref[r, 2 * i + 1]][:, 0 : quarter - block]
        return carry

    lax.fori_loop(0, upd.shape[0], place, 0)
    last = pltpu.make_async_copy(upd, upd_out, sem.at[4 * SPLIT])
    last.start()
    for copy in copies:
        copy.wait()
    last.wait()


def per_device(grads, owner_table, momentum, second, left_stat, right_stat, left_root, right_root):
    groups, shards = lax.axis_size("replica"), lax.axis_size("shard")
    _, rb, rows_dev, full_width = grads.shape
    block = left_stat.shape[2]
    quarter = full_width // groups
    n = CHUNKS
    width = block // n
    cfg = (groups, shards, rb, rows_dev, quarter, block, n, width)
    sq = (block, block)
    whole = pltpu.VMEM((2, rb, rows_dev, width), BF16)
    halves = pltpu.VMEM((2, rb // 2, rows_dev, width), BF16)
    slots = pltpu.VMEM((shards, rows_dev, width), BF16)
    wide_slots = pltpu.VMEM((shards, rows_dev, block), BF16)
    dma = pltpu.SemaphoreType.DMA
    hbm = pl.BlockSpec(memory_space=pltpu.HBM)
    vmem = pl.BlockSpec(memory_space=pltpu.VMEM)
    operands = (owner_table, grads[0], *[a[0, 0] for a in (momentum, second, left_stat, right_stat, left_root, right_root)])
    results = pl.pallas_call(
        functools.partial(kernel, cfg),
        name="shampoo_step",
        out_shape=(pltpu.VMEM((shards, rows_dev, block), BF16),) + (pltpu.VMEM(sq, F32),) * 4,
        in_specs=[hbm] * 8,
        out_specs=[vmem] * 5,
        scratch_shapes=[whole] * (3 * n)
        + [halves] * (2 * n)
        + [whole]
        + [slots] * (2 * n)
        + [pltpu.VMEM(sq, F32)] * 2
        + [pltpu.VMEM(sq, BF16)] * 3
        + [pltpu.VMEM(sq, F32), wide_slots, pltpu.VMEM((rb, rows_dev, full_width), BF16)]
        + [pltpu.VMEM(owner_table.shape, jnp.int32), pltpu.VMEM((1, 128), jnp.int32), pltpu.SMEM((1, 128), jnp.int32)]
        + [dma((6,)), dma((4, 3)), dma((2,)), dma((3, 2)), dma((3, 2)), dma((3, 2, n, 2)), dma((3, 2, n, 2)), dma((n,)), dma((n,)), dma, dma] + [pltpu.SemaphoreType.REGULAR] * 3,
        compiler_params=pltpu.CompilerParams(collective_id=1, has_side_effects=True, vmem_limit_bytes=40 * 2**20),
        cost_estimate=pl.CostEstimate(flops=8 * block**3, bytes_accessed=16 * 2**20, transcendentals=0),
    )(*[pltpu.with_memory_space_constraint(a, pltpu.HBM) for a in operands])
    update, moment_new, second_new, left_new, right_new = pl.pallas_call(
        functools.partial(finish, quarter, block),
        name="place_update",
        out_shape=(jax.ShapeDtypeStruct((rb, rows_dev, quarter), BF16),) + (jax.ShapeDtypeStruct(sq, F32),) * 4,
        in_specs=[hbm] + [vmem] * 5,
        out_specs=[hbm] * 5,
        scratch_shapes=[pltpu.VMEM((rb, rows_dev, quarter), BF16), pltpu.SMEM(owner_table.shape, jnp.int32), dma((4 * SPLIT + 1,)), dma],
        compiler_params=pltpu.CompilerParams(vmem_limit_bytes=8 * 2**20),
    )(pltpu.with_memory_space_constraint(owner_table, pltpu.HBM), *results)
    shape_own = (1, 1, block, block)
    return (
        update,
        moment_new.reshape(shape_own),
        second_new.reshape(shape_own),
        left_new.reshape(shape_own),
        right_new.reshape(shape_own),
    )


def solution(mesh):
    owned = P("replica", "shard", None, None)
    return jax.shard_map(
        per_device,
        mesh=mesh,
        in_specs=(P("replica", None, "shard", None), P(), owned, owned, owned, owned, owned, owned),
        out_specs=(P(None, "shard", "replica"), owned, owned, owned, owned),
        check_vma=False,
    )
```

```python
import functools

import jax
import jax.numpy as jnp
from jax import lax
from jax.experimental import pallas as pl
from jax.experimental.pallas import tpu as pltpu
from jax.sharding import PartitionSpec as P

BETA_STAT = 0.95
BETA_SECOND = 0.99
BETA_MOMENT = 0.9
EPS_ADAM = 1e-08
EPS_NORM = 1e-06
LEARN_RATE = 0.5
MESH = pl.DeviceIdType.MESH
F32 = jnp.float32
BF16 = jnp.bfloat16
CHUNKS = 4
SPOTS = 8
SPLIT = 1


def kernel(cfg, table_in, g_in, mom_in, sec_in, ls_in, rs_in, lr_in, rr_in, back_arrived, mom, sec, ls, rs, *scratch):
    groups, shards, rb, rows_dev, quarter, block, n, width = cfg
    half = rb // 2
    scratch = list(scratch)

    def take(count):
        got = scratch[:count]
        del scratch[:count]
        return got

    from_next, from_prev, total = take(n), take(n), take(n)
    relay = [take(2) for _ in range(n)]
    (from_opp,) = take(1)
    out_p, arrived = take(n), take(n)
    lr, rr, lroot, rroot, gb, shaped, back, g_ref, table_ref, inv_v, inv_ref = take(11)
    in_sem, g_sem, inv_sem, d_send, d_recv, y_send, y_recv, a_send, a_recv, b_send, b_recv, near_in, line_in, all_in = take(14)

    r, s = lax.axis_index("replica"), lax.axis_index("shard")
    nxt, prv, opp = lax.rem(r + 1, groups), lax.rem(r + groups - 1, groups), lax.rem(r + 2, groups)

    barrier = pltpu.get_barrier_semaphore()
    plane, spot, planes = lax.div(s, SPOTS), lax.rem(s, SPOTS), shards // SPOTS
    in_plane = [(r, plane * SPOTS + lax.rem(spot + k, SPOTS)) for k in range(1, SPOTS)]
    in_line = [(r, lax.rem(plane + k, planes) * SPOTS + spot) for k in range(planes)]
    near = [(nxt, s), (prv, s), (opp, s), in_line[1], in_line[planes - 1]] + in_plane
    def greet(peers):
        for peer in peers:
            pl.semaphore_signal(barrier, inc=1, device_id=peer, device_id_type=MESH)

    greet(near[:3])

    early, late = n - 1, list(range(n - 1))
    spans = [(early * width, width), (0, early * width), (block, quarter - block)]

    def load(i, q, k):
        lo, wide = spans[k]
        at = pl.ds(pl.multiple_of(q * quarter + lo, 128), wide)
        return pltpu.make_async_copy(g_in.at[:, :, at], g_ref.at[:, :, at], g_sem.at[i, k])

    loads = [[load(i, q, k) for k in range(3)] for i, q in enumerate((opp, nxt, prv, r))]
    for i in range(3):
        loads[i][0].start()
    greet(near[3:])
    for i in range(4):
        for k in range(1 if i < 3 else 0, 3):
            loads[i][k].start()
    table_copy = pltpu.make_async_copy(table_in, table_ref, inv_sem.at[0])
    table_copy.start()
    def part(j, c):
        start = c * block + j * width
        return start, max(0, min(width, quarter - start))

    def piece(q, lo, rows, j, c):
        start, wide = part(j, c)
        return g_ref.at[pl.ds(lo, rows), :, pl.ds(pl.multiple_of(q * quarter + start, 128), wide)]

    parts = [(j, c) for j in range(n) for c in range(2) if part(j, c)[1] > 0]
    for j in range(n):
        wide = part(j, 1)[1]
        if wide < width:
            total[j][1, :, :, wide:] = jnp.zeros((rb, rows_dev, width - wide), BF16)
    def y_copy(kind, way, j, c, src, dst):
        return pltpu.make_async_remote_copy(
            src_ref=src,
            dst_ref=dst,
            send_sem=y_send.at[kind, way, j, c],
            recv_sem=y_recv.at[kind, way, j, c],
            device_id=(nxt if way else prv, s),
            device_id_type=MESH,
        )

    first, direct, onward = {}, {}, {}
    for j, c in parts:
        if j == n - 1:
            continue
        wide = pl.ds(0, part(j, c)[1])
        lower, upper = pl.ds(0, half), pl.ds(half, half)
        first[j, c] = [
            y_copy(0, 0, j, c, piece(opp, 0, half, j, c), relay[j][0].at[c, :, :, wide]),
            y_copy(0, 1, j, c, piece(opp, half, half, j, c), relay[j][1].at[c, :, :, wide]),
        ]
        direct[j, c] = [
            y_copy(1, 0, j, c, piece(prv, half, half, j, c), from_next[j].at[c, upper, :, wide]),
            y_copy(1, 1, j, c, piece(nxt, 0, half, j, c), from_prev[j].at[c, lower, :, wide]),
        ]
        onward[j, c] = [
            y_copy(2, 0, j, c, relay[j][0].at[c, :, :, wide], from_next[j].at[c, lower, :, wide]),
            y_copy(2, 1, j, c, relay[j][1].at[c, :, :, wide], from_prev[j].at[c, upper, :, wide]),
        ]

    straight = [
        pltpu.make_async_remote_copy(
            src_ref=piece(q, 0, rb, early, c),
            dst_ref=buf.at[c, :, :, pl.ds(0, part(early, c)[1])],
            send_sem=d_send.at[i, c],
            recv_sem=d_recv.at[i, c],
            device_id=(q, s),
            device_id_type=MESH,
        )
        for i, (q, buf) in enumerate(((opp, from_opp), (nxt, from_prev[early]), (prv, from_next[early])))
        for c in range(2)
        if part(early, c)[1]
    ]

    def start(table, j):
        if j < n:
            for c in range(2):
                for copy in table.get((j, c), ()):
                    copy.start()

    def tell(peers, sem):
        for peer in peers:
            pl.semaphore_signal(sem, inc=1, device_id=peer, device_id_type=MESH)

    for i in range(3):
        loads[i][0].wait()
    pl.semaphore_wait(barrier, len(near))
    tell((in_line[1], in_line[planes - 1]), near_in)
    for copy in straight:
        copy.start()
    for copy in loads[0][1:]:
        copy.wait()
    for j in late:
        start(first, j)
    for copy in loads[1][1:] + loads[2][1:]:
        copy.wait()
    start(direct, 0)
    for copy in loads[3]:
        copy.wait()
    table_copy.wait()
    table = table_ref[pl.ds(r, 1), :]
    rows = lax.broadcasted_iota(jnp.int32, (shards, shards), 0)
    cols = lax.broadcasted_iota(jnp.int32, (shards, shards), 1)
    column = jnp.sum(jnp.where(rows == cols, table, 0), axis=1, keepdims=True)
    inv_v[...] = jnp.zeros_like(inv_v)
    inv_v[:, 0:shards] = jnp.max(jnp.where(column == cols, rows, 0), axis=0, keepdims=True)
    inv_copy = pltpu.make_async_copy(inv_v, inv_ref, inv_sem.at[1])
    inv_copy.start()

    pl.semaphore_wait(near_in, 2)
    tell((in_line[2], in_line[planes - 2]), line_in)
    pl.semaphore_wait(line_in, 2)
    tell(in_plane, all_in)

    in_copies = [
        pltpu.make_async_copy(src, dst, in_sem.at[i])
        for i, (src, dst) in enumerate(((lr_in, lr), (rr_in, rr), (sec_in, sec), (mom_in, mom), (ls_in, ls), (rs_in, rs)))
    ]
    for copy in in_copies:
        copy.start()

    tile = 128

    def mine(q, lo, count, j, c):
        start, wide = part(j, c)
        return g_ref[pl.ds(lo, count), :, pl.ds(pl.multiple_of(q * quarter + start, 128), wide)].astype(F32)

    def pass_on(j):
        for c in range(2):
            wide = part(j, c)[1]
            for way, q, lo in ((0, prv, 0), (1, nxt, half)) if wide else ():
                first[j, c][way].wait_recv()
                buf = relay[j][way]
                buf[c, :, :, 0:wide] = (buf[c, :, :, 0:wide].astype(F32) + mine(q, lo, half, j, c)).astype(BF16)
                onward[j, c][way].start()

    def target(k):
        turn, spot_k = lax.div(k, SPOTS), lax.rem(k, SPOTS)
        far = lax.div(turn + 1, 2)
        off = planes // 2 + far * (1 - 2 * lax.rem(turn, 2))
        return lax.rem(plane + off, planes) * SPOTS + lax.rem(spot + 1 + spot_k, SPOTS)

    def hand_out(j):
        if j == early:
            for copy in straight:
                copy.wait_recv()
        for c in range(2):
            wide = part(j, c)[1]
            if not wide:
                continue
            if j != early:
                for way in range(2):
                    direct[j, c][way].wait_recv()
                    onward[j, c][way].wait_recv()
            summed = mine(r, 0, rb, j, c) + from_next[j][c, :, :, 0:wide].astype(F32) + from_prev[j][c, :, :, 0:wide].astype(F32)
            if j == early:
                summed = summed + from_opp[c, :, :, 0:wide].astype(F32)
            total[j][c, :, :, 0:wide] = summed.astype(BF16)

        def block_of(d):
            b = inv_ref[0, d]
            return total[j][lax.rem(b, 2), lax.div(b, 2)]

        def send(k, carry):
            d = target(k)
            out_p[j][d] = block_of(d)
            pltpu.make_async_remote_copy(
                src_ref=out_p[j].at[d],
                dst_ref=arrived[j].at[s],
                send_sem=a_send.at[j],
                recv_sem=a_recv.at[j],
                device_id=(r, d),
                device_id_type=MESH,
            ).start()
            return carry

        lax.fori_loop(0, shards - 1, send, 0, unroll=9)
        arrived[j][s] = block_of(s)

    def others(src, dst, sem):
        return pltpu.make_async_copy(src.at[pl.ds(0, shards - 1)], dst.at[pl.ds(0, shards - 1)], sem)

    inv_copy.wait()
    for j in late:
        pass_on(j)
        start(direct, j + 1)
        if j == min(1, late[-1]):
            pl.semaphore_wait(all_in, len(in_plane))
            hand_out(early)
    for j in late:
        hand_out(j)

    for copy in in_copies[:2]:
        copy.wait()

    def cast_roots(t, carry):
        at = pl.ds(pl.multiple_of(t * tile, tile), tile)
        lroot[at, :] = lr[at, :].astype(BF16)
        rroot[at, :] = rr[at, :].astype(BF16)
        return carry

    lax.fori_loop(0, block // tile, cast_roots, 0)

    for copy in in_copies[2:]:
        copy.wait()
    own_c = lax.rem(inv_ref[0, s], 2)
    real = quarter - own_c * block
    chunk_rows = 64
    adam_sq = jnp.zeros((8, width), F32)
    shaped_sq = jnp.zeros((8, block), F32)
    for j in [early] + late:
        others(out_p[j], arrived[j], a_recv.at[j]).wait()
        cols = slice(j * width, (j + 1) * width)

        def second_step(t, acc):
            at = pl.ds(pl.multiple_of(t * chunk_rows, chunk_rows), chunk_rows)
            g = arrived[j][pl.ds(pl.multiple_of(t * (chunk_rows // 8), 8), chunk_rows // 8)].astype(F32).reshape(chunk_rows, width)
            gb[at, cols] = g.astype(BF16)
            second = BETA_SECOND * sec[at, cols] + (1.0 - BETA_SECOND) * g * g
            sec[at, cols] = second
            adam = g / (jnp.sqrt(second) + EPS_ADAM)
            return acc + jnp.sum((adam * adam).reshape(chunk_rows // 8, 8, width), axis=0)

        adam_sq = lax.fori_loop(0, block // chunk_rows, second_step, adam_sq, unroll=True)

        def shape_step(t, acc):
            at = pl.ds(pl.multiple_of(t * tile, tile), tile)
            left = jnp.dot(lroot[at, :], gb[:, cols], preferred_element_type=F32).astype(BF16)
            both = jnp.dot(left, rroot[cols, :], preferred_element_type=F32)
            if j != early:
                both = both + shaped[at, :]
            if j == late[-1]:
                both = jnp.where(lax.broadcasted_iota(jnp.int32, (tile, block), 1) < real, both, 0.0)
                acc = acc + jnp.sum((both * both).reshape(tile // 8, 8, block), axis=0)
            shaped[at, :] = both
            return acc

        shaped_sq = lax.fori_loop(0, block // tile, shape_step, shaped_sq, unroll=True)

    adam_norm = jnp.sum(jnp.sum(adam_sq, axis=0, keepdims=True), axis=1, keepdims=True)
    shaped_norm = jnp.sum(jnp.sum(shaped_sq, axis=0, keepdims=True), axis=1, keepdims=True)
    scale = jnp.sqrt(adam_norm + EPS_NORM) / jnp.sqrt(shaped_norm + EPS_NORM)

    per = chunk_rows // 8
    turns = shards // per

    def moment_step(k, carry):
        far = lax.div(k + 1, 2)
        t = lax.rem(lax.div(s, per) + turns // 2 + far * (1 - 2 * lax.rem(k, 2)), turns)
        at = pl.ds(pl.multiple_of(t * chunk_rows, chunk_rows), chunk_rows)
        moment = BETA_MOMENT * mom[at, :] + scale * shaped[at, :]
        mom[at, :] = moment
        back[pl.ds(pl.multiple_of(t * per, per), per)] = (-LEARN_RATE * moment).reshape(per, 8, block).astype(BF16)
        for i in range(per):
            d = t * per + i

            @pl.when(d != s)
            def _():
                pltpu.make_async_remote_copy(
                    src_ref=back.at[d],
                    dst_ref=back_arrived.at[s],
                    send_sem=b_send,
                    recv_sem=b_recv,
                    device_id=(r, d),
                    device_id_type=MESH,
                ).start()

        return carry

    lax.fori_loop(0, turns, moment_step, 0, unroll=True)
    back_arrived[s] = back[s]

    def left_step(t, carry):
        at = pl.ds(pl.multiple_of(t * tile, tile), tile)
        gram = lax.dot_general(gb[at, :], gb[...], (((1,), (1,)), ((), ())), preferred_element_type=F32)
        ls[at, :] = BETA_STAT * ls[at, :] + (1.0 - BETA_STAT) * gram
        return carry

    lax.fori_loop(0, block // tile, left_step, 0)

    for t in range(block // tile):
        at = slice(t * tile, (t + 1) * tile)
        gram = lax.dot_general(gb[:, at], gb[...], (((0,), (0,)), ((), ())), preferred_element_type=F32)
        rs[at, :] = BETA_STAT * rs[at, :] + (1.0 - BETA_STAT) * gram

    others(back, back_arrived, b_recv).wait()

    for copy in straight:
        copy.wait_send()
    for table in (first, direct, onward):
        for pair in table.values():
            for copy in pair:
                copy.wait_send()
    for j in range(n):
        others(out_p[j], arrived[j], a_send.at[j]).wait()
    others(back, back_arrived, b_send).wait()


def finish(quarter, block, table_in, arrived, mom, sec, ls, rs, upd_out, mom_out, sec_out, left_out, right_out, upd, table_ref, sem, table_sem):
    table_copy = pltpu.make_async_copy(table_in, table_ref, table_sem)
    table_copy.start()
    pairs = ((mom, mom_out), (sec, sec_out), (ls, left_out), (rs, right_out))
    rows = block // SPLIT
    copies = [
        pltpu.make_async_copy(src.at[pl.ds(k * rows, rows)], dst.at[pl.ds(k * rows, rows)], sem.at[i * SPLIT + k])
        for i, (src, dst) in enumerate(pairs)
        for k in range(SPLIT)
    ]
    for copy in copies:
        copy.start()

    r = lax.axis_index("replica")
    table_copy.wait()

    def place(i, carry):
        upd[i, :, 0:block] = arrived[table_ref[r, 2 * i]]
        upd[i, :, block:quarter] = arrived[table_ref[r, 2 * i + 1]][:, 0 : quarter - block]
        return carry

    lax.fori_loop(0, upd.shape[0], place, 0)
    last = pltpu.make_async_copy(upd, upd_out, sem.at[4 * SPLIT])
    last.start()
    for copy in copies:
        copy.wait()
    last.wait()


def per_device(grads, owner_table, momentum, second, left_stat, right_stat, left_root, right_root):
    groups, shards = lax.axis_size("replica"), lax.axis_size("shard")
    _, rb, rows_dev, full_width = grads.shape
    block = left_stat.shape[2]
    quarter = full_width // groups
    n = CHUNKS
    width = block // n
    cfg = (groups, shards, rb, rows_dev, quarter, block, n, width)
    sq = (block, block)
    whole = pltpu.VMEM((2, rb, rows_dev, width), BF16)
    halves = pltpu.VMEM((2, rb // 2, rows_dev, width), BF16)
    slots = pltpu.VMEM((shards, rows_dev, width), BF16)
    wide_slots = pltpu.VMEM((shards, rows_dev, block), BF16)
    dma = pltpu.SemaphoreType.DMA
    hbm = pl.BlockSpec(memory_space=pltpu.HBM)
    vmem = pl.BlockSpec(memory_space=pltpu.VMEM)
    operands = (owner_table, grads[0], *[a[0, 0] for a in (momentum, second, left_stat, right_stat, left_root, right_root)])
    results = pl.pallas_call(
        functools.partial(kernel, cfg),
        name="shampoo_step",
        out_shape=(pltpu.VMEM((shards, rows_dev, block), BF16),) + (pltpu.VMEM(sq, F32),) * 4,
        in_specs=[hbm] * 8,
        out_specs=[vmem] * 5,
        scratch_shapes=[whole] * (3 * n)
        + [halves] * (2 * n)
        + [whole]
        + [slots] * (2 * n)
        + [pltpu.VMEM(sq, F32)] * 2
        + [pltpu.VMEM(sq, BF16)] * 3
        + [pltpu.VMEM(sq, F32), wide_slots, pltpu.VMEM((rb, rows_dev, full_width), BF16)]
        + [pltpu.VMEM(owner_table.shape, jnp.int32), pltpu.VMEM((1, 128), jnp.int32), pltpu.SMEM((1, 128), jnp.int32)]
        + [dma((6,)), dma((4, 3)), dma((2,)), dma((3, 2)), dma((3, 2)), dma((3, 2, n, 2)), dma((3, 2, n, 2)), dma((n,)), dma((n,)), dma, dma] + [pltpu.SemaphoreType.REGULAR] * 3,
        compiler_params=pltpu.CompilerParams(collective_id=1, has_side_effects=True, vmem_limit_bytes=40 * 2**20),
        cost_estimate=pl.CostEstimate(flops=8 * block**3, bytes_accessed=16 * 2**20, transcendentals=0),
    )(*[pltpu.with_memory_space_constraint(a, pltpu.HBM) for a in operands])
    update, moment_new, second_new, left_new, right_new = pl.pallas_call(
        functools.partial(finish, quarter, block),
        name="place_update",
        out_shape=(jax.ShapeDtypeStruct((rb, rows_dev, quarter), BF16),) + (jax.ShapeDtypeStruct(sq, F32),) * 4,
        in_specs=[hbm] + [vmem] * 5,
        out_specs=[hbm] * 5,
        scratch_shapes=[pltpu.VMEM((rb, rows_dev, quarter), BF16), pltpu.SMEM(owner_table.shape, jnp.int32), dma((4 * SPLIT + 1,)), dma],
        compiler_params=pltpu.CompilerParams(vmem_limit_bytes=8 * 2**20),
    )(pltpu.with_memory_space_constraint(owner_table, pltpu.HBM), *results)
    shape_own = (1, 1, block, block)
    return (
        update,
        moment_new.reshape(shape_own),
        second_new.reshape(shape_own),
        left_new.reshape(shape_own),
        right_new.reshape(shape_own),
    )


def solution(mesh):
    owned = P("replica", "shard", None, None)
    return jax.shard_map(
        per_device,
        mesh=mesh,
        in_specs=(P("replica", None, "shard", None), P(), owned, owned, owned, owned, owned, owned),
        out_specs=(P(None, "shard", "replica"), owned, owned, owned, owned),
        check_vma=False,
    )
```

```python
import functools

import jax
import jax.numpy as jnp
from jax import lax
from jax.experimental import pallas as pl
from jax.experimental.pallas import tpu as pltpu
from jax.sharding import PartitionSpec as P

BETA_STAT = 0.95
BETA_SECOND = 0.99
BETA_MOMENT = 0.9
EPS_ADAM = 1e-08
EPS_NORM = 1e-06
LEARN_RATE = 0.5
MESH = pl.DeviceIdType.MESH
F32 = jnp.float32
BF16 = jnp.bfloat16
CHUNKS = 4
SPOTS = 8
SPLIT = 1


def kernel(cfg, table_in, g_in, mom_in, sec_in, ls_in, rs_in, lr_in, rr_in, back_arrived, mom, sec, ls, rs, *scratch):
    groups, shards, rb, rows_dev, quarter, block, n, width = cfg
    half = rb // 2
    scratch = list(scratch)

    def take(count):
        got = scratch[:count]
        del scratch[:count]
        return got

    from_next, from_prev, total = take(n), take(n), take(n)
    relay = [take(2) for _ in range(n)]
    (from_opp,) = take(1)
    out_p, arrived = take(n), take(n)
    lr, rr, lroot, rroot, gb, shaped, back, g_ref, table_ref, inv_v, inv_ref = take(11)
    in_sem, g_sem, inv_sem, d_send, d_recv, y_send, y_recv, a_send, a_recv, b_send, b_recv, near_in, line_in, all_in = take(14)

    r, s = lax.axis_index("replica"), lax.axis_index("shard")
    nxt, prv, opp = lax.rem(r + 1, groups), lax.rem(r + groups - 1, groups), lax.rem(r + 2, groups)

    barrier = pltpu.get_barrier_semaphore()
    plane, spot, planes = lax.div(s, SPOTS), lax.rem(s, SPOTS), shards // SPOTS
    in_plane = [(r, plane * SPOTS + lax.rem(spot + k, SPOTS)) for k in range(1, SPOTS)]
    in_line = [(r, lax.rem(plane + k, planes) * SPOTS + spot) for k in range(planes)]
    near = [(nxt, s), (prv, s), (opp, s), in_line[1], in_line[planes - 1]] + in_plane
    def greet(peers):
        for peer in peers:
            pl.semaphore_signal(barrier, inc=1, device_id=peer, device_id_type=MESH)

    greet(near[:3])

    early, late = n - 1, list(range(n - 1))
    spans = [(early * width, width), (0, early * width), (block, quarter - block)]

    def load(i, q, k):
        lo, wide = spans[k]
        at = pl.ds(pl.multiple_of(q * quarter + lo, 128), wide)
        return pltpu.make_async_copy(g_in.at[:, :, at], g_ref.at[:, :, at], g_sem.at[i, k])

    loads = [[load(i, q, k) for k in range(3)] for i, q in enumerate((opp, nxt, prv, r))]
    for i in range(3):
        loads[i][0].start()
    greet(near[3:])
    for i in range(4):
        for k in range(1 if i < 3 else 0, 3):
            loads[i][k].start()
    table_copy = pltpu.make_async_copy(table_in, table_ref, inv_sem.at[0])
    table_copy.start()
    def part(j, c):
        start = c * block + j * width
        return start, max(0, min(width, quarter - start))

    def piece(q, lo, rows, j, c):
        start, wide = part(j, c)
        return g_ref.at[pl.ds(lo, rows), :, pl.ds(pl.multiple_of(q * quarter + start, 128), wide)]

    parts = [(j, c) for j in range(n) for c in range(2) if part(j, c)[1] > 0]
    for j in range(n):
        wide = part(j, 1)[1]
        if wide < width:
            total[j][1, :, :, wide:] = jnp.zeros((rb, rows_dev, width - wide), BF16)
    def y_copy(kind, way, j, c, src, dst):
        return pltpu.make_async_remote_copy(
            src_ref=src,
            dst_ref=dst,
            send_sem=y_send.at[kind, way, j, c],
            recv_sem=y_recv.at[kind, way, j, c],
            device_id=(nxt if way else prv, s),
            device_id_type=MESH,
        )

    first, direct, onward = {}, {}, {}
    for j, c in parts:
        if j == n - 1:
            continue
        wide = pl.ds(0, part(j, c)[1])
        lower, upper = pl.ds(0, half), pl.ds(half, half)
        first[j, c] = [
            y_copy(0, 0, j, c, piece(opp, 0, half, j, c), relay[j][0].at[c, :, :, wide]),
            y_copy(0, 1, j, c, piece(opp, half, half, j, c), relay[j][1].at[c, :, :, wide]),
        ]
        direct[j, c] = [
            y_copy(1, 0, j, c, piece(prv, half, half, j, c), from_next[j].at[c, upper, :, wide]),
            y_copy(1, 1, j, c, piece(nxt, 0, half, j, c), from_prev[j].at[c, lower, :, wide]),
        ]
        onward[j, c] = [
            y_copy(2, 0, j, c, relay[j][0].at[c, :, :, wide], from_next[j].at[c, lower, :, wide]),
            y_copy(2, 1, j, c, relay[j][1].at[c, :, :, wide], from_prev[j].at[c, upper, :, wide]),
        ]

    straight = [
        pltpu.make_async_remote_copy(
            src_ref=piece(q, 0, rb, early, c),
            dst_ref=buf.at[c, :, :, pl.ds(0, part(early, c)[1])],
            send_sem=d_send.at[i, c],
            recv_sem=d_recv.at[i, c],
            device_id=(q, s),
            device_id_type=MESH,
        )
        for i, (q, buf) in enumerate(((opp, from_opp), (nxt, from_prev[early]), (prv, from_next[early])))
        for c in range(2)
        if part(early, c)[1]
    ]

    def start(table, j):
        if j < n:
            for c in range(2):
                for copy in table.get((j, c), ()):
                    copy.start()

    def tell(peers, sem):
        for peer in peers:
            pl.semaphore_signal(sem, inc=1, device_id=peer, device_id_type=MESH)

    for i in range(3):
        loads[i][0].wait()
    pl.semaphore_wait(barrier, len(near))
    tell((in_line[1], in_line[planes - 1]), near_in)
    for copy in straight:
        copy.start()
    for copy in loads[0][1:]:
        copy.wait()
    for j in late:
        start(first, j)
    for copy in loads[1][1:] + loads[2][1:]:
        copy.wait()
    start(direct, 0)
    for copy in loads[3]:
        copy.wait()
    table_copy.wait()
    table = table_ref[pl.ds(r, 1), :]
    rows = lax.broadcasted_iota(jnp.int32, (shards, shards), 0)
    cols = lax.broadcasted_iota(jnp.int32, (shards, shards), 1)
    column = jnp.sum(jnp.where(rows == cols, table, 0), axis=1, keepdims=True)
    inv_v[...] = jnp.zeros_like(inv_v)
    inv_v[:, 0:shards] = jnp.max(jnp.where(column == cols, rows, 0), axis=0, keepdims=True)
    inv_copy = pltpu.make_async_copy(inv_v, inv_ref, inv_sem.at[1])
    inv_copy.start()

    pl.semaphore_wait(near_in, 2)
    tell((in_line[2], in_line[planes - 2]), line_in)
    pl.semaphore_wait(line_in, 2)
    tell(in_plane, all_in)

    in_copies = [
        pltpu.make_async_copy(src, dst, in_sem.at[i])
        for i, (src, dst) in enumerate(((lr_in, lr), (rr_in, rr), (sec_in, sec), (mom_in, mom), (ls_in, ls), (rs_in, rs)))
    ]
    for copy in in_copies:
        copy.start()

    tile = 128

    def mine(q, lo, count, j, c):
        start, wide = part(j, c)
        return g_ref[pl.ds(lo, count), :, pl.ds(pl.multiple_of(q * quarter + start, 128), wide)].astype(F32)

    def pass_on(j):
        for c in range(2):
            wide = part(j, c)[1]
            for way, q, lo in ((0, prv, 0), (1, nxt, half)) if wide else ():
                first[j, c][way].wait_recv()
                buf = relay[j][way]
                buf[c, :, :, 0:wide] = (buf[c, :, :, 0:wide].astype(F32) + mine(q, lo, half, j, c)).astype(BF16)
                onward[j, c][way].start()

    def target(k):
        turn, spot_k = lax.div(k, SPOTS), lax.rem(k, SPOTS)
        far = lax.div(turn + 1, 2)
        off = planes // 2 + far * (1 - 2 * lax.rem(turn, 2))
        return lax.rem(plane + off, planes) * SPOTS + lax.rem(spot + 1 + spot_k, SPOTS)

    def hand_out(j):
        if j == early:
            for copy in straight:
                copy.wait_recv()
        for c in range(2):
            wide = part(j, c)[1]
            if not wide:
                continue
            if j != early:
                for way in range(2):
                    direct[j, c][way].wait_recv()
                    onward[j, c][way].wait_recv()
            summed = mine(r, 0, rb, j, c) + from_next[j][c, :, :, 0:wide].astype(F32) + from_prev[j][c, :, :, 0:wide].astype(F32)
            if j == early:
                summed = summed + from_opp[c, :, :, 0:wide].astype(F32)
            total[j][c, :, :, 0:wide] = summed.astype(BF16)

        def block_of(d):
            b = inv_ref[0, d]
            return total[j][lax.rem(b, 2), lax.div(b, 2)]

        def send(k, carry):
            d = target(k)
            out_p[j][d] = block_of(d)
            pltpu.make_async_remote_copy(
                src_ref=out_p[j].at[d],
                dst_ref=arrived[j].at[s],
                send_sem=a_send.at[j],
                recv_sem=a_recv.at[j],
                device_id=(r, d),
                device_id_type=MESH,
            ).start()
            return carry

        lax.fori_loop(0, shards - 1, send, 0, unroll=9)
        arrived[j][s] = block_of(s)

    def others(src, dst, sem):
        return pltpu.make_async_copy(src.at[pl.ds(0, shards - 1)], dst.at[pl.ds(0, shards - 1)], sem)

    inv_copy.wait()
    for j in late:
        pass_on(j)
        start(direct, j + 1)
        if j == min(1, late[-1]):
            pl.semaphore_wait(all_in, len(in_plane))
            hand_out(early)
    for j in late:
        hand_out(j)

    for copy in in_copies[:2]:
        copy.wait()

    def cast_roots(t, carry):
        at = pl.ds(pl.multiple_of(t * tile, tile), tile)
        lroot[at, :] = lr[at, :].astype(BF16)
        rroot[at, :] = rr[at, :].astype(BF16)
        return carry

    lax.fori_loop(0, block // tile, cast_roots, 0)

    for copy in in_copies[2:]:
        copy.wait()
    own_c = lax.rem(inv_ref[0, s], 2)
    real = quarter - own_c * block
    chunk_rows = 64
    adam_sq = jnp.zeros((8, width), F32)
    shaped_sq = jnp.zeros((8, block), F32)
    for j in [early] + late:
        others(out_p[j], arrived[j], a_recv.at[j]).wait()
        cols = slice(j * width, (j + 1) * width)

        def second_step(t, acc):
            at = pl.ds(pl.multiple_of(t * chunk_rows, chunk_rows), chunk_rows)
            g = arrived[j][pl.ds(pl.multiple_of(t * (chunk_rows // 8), 8), chunk_rows // 8)].astype(F32).reshape(chunk_rows, width)
            gb[at, cols] = g.astype(BF16)
            second = BETA_SECOND * sec[at, cols] + (1.0 - BETA_SECOND) * g * g
            sec[at, cols] = second
            adam = g / (jnp.sqrt(second) + EPS_ADAM)
            return acc + jnp.sum((adam * adam).reshape(chunk_rows // 8, 8, width), axis=0)

        adam_sq = lax.fori_loop(0, block // chunk_rows, second_step, adam_sq, unroll=True)

        def shape_step(t, acc):
            at = pl.ds(pl.multiple_of(t * tile, tile), tile)
            left = jnp.dot(lroot[at, :], gb[:, cols], preferred_element_type=F32).astype(BF16)
            both = jnp.dot(left, rroot[cols, :], preferred_element_type=F32)
            if j != early:
                both = both + shaped[at, :]
            if j == late[-1]:
                both = jnp.where(lax.broadcasted_iota(jnp.int32, (tile, block), 1) < real, both, 0.0)
                acc = acc + jnp.sum((both * both).reshape(tile // 8, 8, block), axis=0)
            shaped[at, :] = both
            return acc

        shaped_sq = lax.fori_loop(0, block // tile, shape_step, shaped_sq, unroll=True)

    adam_norm = jnp.sum(jnp.sum(adam_sq, axis=0, keepdims=True), axis=1, keepdims=True)
    shaped_norm = jnp.sum(jnp.sum(shaped_sq, axis=0, keepdims=True), axis=1, keepdims=True)
    scale = jnp.sqrt(adam_norm + EPS_NORM) / jnp.sqrt(shaped_norm + EPS_NORM)

    per = chunk_rows // 8
    turns = shards // per

    def moment_step(k, carry):
        far = lax.div(k + 1, 2)
        t = lax.rem(lax.div(s, per) + turns // 2 + far * (1 - 2 * lax.rem(k, 2)), turns)
        at = pl.ds(pl.multiple_of(t * chunk_rows, chunk_rows), chunk_rows)
        moment = BETA_MOMENT * mom[at, :] + scale * shaped[at, :]
        mom[at, :] = moment
        back[pl.ds(pl.multiple_of(t * per, per), per)] = (-LEARN_RATE * moment).reshape(per, 8, block).astype(BF16)
        for i in range(per):
            d = t * per + i

            @pl.when(d != s)
            def _():
                pltpu.make_async_remote_copy(
                    src_ref=back.at[d],
                    dst_ref=back_arrived.at[s],
                    send_sem=b_send,
                    recv_sem=b_recv,
                    device_id=(r, d),
                    device_id_type=MESH,
                ).start()

        return carry

    lax.fori_loop(0, turns, moment_step, 0, unroll=True)
    back_arrived[s] = back[s]

    def left_step(t, carry):
        at = pl.ds(pl.multiple_of(t * tile, tile), tile)
        gram = lax.dot_general(gb[at, :], gb[...], (((1,), (1,)), ((), ())), preferred_element_type=F32)
        ls[at, :] = BETA_STAT * ls[at, :] + (1.0 - BETA_STAT) * gram
        return carry

    lax.fori_loop(0, block // tile, left_step, 0)

    for t in range(block // tile):
        at = slice(t * tile, (t + 1) * tile)
        gram = lax.dot_general(gb[:, at], gb[...], (((0,), (0,)), ((), ())), preferred_element_type=F32)
        rs[at, :] = BETA_STAT * rs[at, :] + (1.0 - BETA_STAT) * gram

    for copy in straight:
        copy.wait_send()
    for table in (first, direct, onward):
        for pair in table.values():
            for copy in pair:
                copy.wait_send()
    for j in range(n):
        others(out_p[j], arrived[j], a_send.at[j]).wait()
    others(back, back_arrived, b_send).wait()
    others(back, back_arrived, b_recv).wait()


def finish(quarter, block, table_in, arrived, mom, sec, ls, rs, upd_out, mom_out, sec_out, left_out, right_out, upd, table_ref, sem, table_sem):
    table_copy = pltpu.make_async_copy(table_in, table_ref, table_sem)
    table_copy.start()
    pairs = ((mom, mom_out), (sec, sec_out), (ls, left_out), (rs, right_out))
    rows = block // SPLIT
    copies = [
        pltpu.make_async_copy(src.at[pl.ds(k * rows, rows)], dst.at[pl.ds(k * rows, rows)], sem.at[i * SPLIT + k])
        for i, (src, dst) in enumerate(pairs)
        for k in range(SPLIT)
    ]
    for copy in copies:
        copy.start()

    r = lax.axis_index("replica")
    table_copy.wait()

    def place(i, carry):
        upd[i, :, 0:block] = arrived[table_ref[r, 2 * i]]
        upd[i, :, block:quarter] = arrived[table_ref[r, 2 * i + 1]][:, 0 : quarter - block]
        return carry

    lax.fori_loop(0, upd.shape[0], place, 0)
    last = pltpu.make_async_copy(upd, upd_out, sem.at[4 * SPLIT])
    last.start()
    for copy in copies:
        copy.wait()
    last.wait()


def per_device(grads, owner_table, momentum, second, left_stat, right_stat, left_root, right_root):
    groups, shards = lax.axis_size("replica"), lax.axis_size("shard")
    _, rb, rows_dev, full_width = grads.shape
    block = left_stat.shape[2]
    quarter = full_width // groups
    n = CHUNKS
    width = block // n
    cfg = (groups, shards, rb, rows_dev, quarter, block, n, width)
    sq = (block, block)
    whole = pltpu.VMEM((2, rb, rows_dev, width), BF16)
    halves = pltpu.VMEM((2, rb // 2, rows_dev, width), BF16)
    slots = pltpu.VMEM((shards, rows_dev, width), BF16)
    wide_slots = pltpu.VMEM((shards, rows_dev, block), BF16)
    dma = pltpu.SemaphoreType.DMA
    hbm = pl.BlockSpec(memory_space=pltpu.HBM)
    vmem = pl.BlockSpec(memory_space=pltpu.VMEM)
    operands = (owner_table, grads[0], *[a[0, 0] for a in (momentum, second, left_stat, right_stat, left_root, right_root)])
    results = pl.pallas_call(
        functools.partial(kernel, cfg),
        name="shampoo_step",
        out_shape=(pltpu.VMEM((shards, rows_dev, block), BF16),) + (pltpu.VMEM(sq, F32),) * 4,
        in_specs=[hbm] * 8,
        out_specs=[vmem] * 5,
        scratch_shapes=[whole] * (3 * n)
        + [halves] * (2 * n)
        + [whole]
        + [slots] * (2 * n)
        + [pltpu.VMEM(sq, F32)] * 2
        + [pltpu.VMEM(sq, BF16)] * 3
        + [pltpu.VMEM(sq, F32), wide_slots, pltpu.VMEM((rb, rows_dev, full_width), BF16)]
        + [pltpu.VMEM(owner_table.shape, jnp.int32), pltpu.VMEM((1, 128), jnp.int32), pltpu.SMEM((1, 128), jnp.int32)]
        + [dma((6,)), dma((4, 3)), dma((2,)), dma((3, 2)), dma((3, 2)), dma((3, 2, n, 2)), dma((3, 2, n, 2)), dma((n,)), dma((n,)), dma, dma] + [pltpu.SemaphoreType.REGULAR] * 3,
        compiler_params=pltpu.CompilerParams(collective_id=1, has_side_effects=True, vmem_limit_bytes=40 * 2**20),
        cost_estimate=pl.CostEstimate(flops=8 * block**3, bytes_accessed=16 * 2**20, transcendentals=0),
    )(*[pltpu.with_memory_space_constraint(a, pltpu.HBM) for a in operands])
    update, moment_new, second_new, left_new, right_new = pl.pallas_call(
        functools.partial(finish, quarter, block),
        name="place_update",
        out_shape=(jax.ShapeDtypeStruct((rb, rows_dev, quarter), BF16),) + (jax.ShapeDtypeStruct(sq, F32),) * 4,
        in_specs=[hbm] + [vmem] * 5,
        out_specs=[hbm] * 5,
        scratch_shapes=[pltpu.VMEM((rb, rows_dev, quarter), BF16), pltpu.SMEM(owner_table.shape, jnp.int32), dma((4 * SPLIT + 1,)), dma],
        compiler_params=pltpu.CompilerParams(vmem_limit_bytes=8 * 2**20),
    )(pltpu.with_memory_space_constraint(owner_table, pltpu.HBM), *results)
    shape_own = (1, 1, block, block)
    return (
        update,
        moment_new.reshape(shape_own),
        second_new.reshape(shape_own),
        left_new.reshape(shape_own),
        right_new.reshape(shape_own),
    )


def solution(mesh):
    owned = P("replica", "shard", None, None)
    return jax.shard_map(
        per_device,
        mesh=mesh,
        in_specs=(P("replica", None, "shard", None), P(), owned, owned, owned, owned, owned, owned),
        out_specs=(P(None, "shard", "replica"), owned, owned, owned, owned),
        check_vma=False,
    )
```

```python
import functools

import jax
import jax.numpy as jnp
from jax import lax
from jax.experimental import pallas as pl
from jax.experimental.pallas import tpu as pltpu
from jax.sharding import PartitionSpec as P

BETA_STAT = 0.95
BETA_SECOND = 0.99
BETA_MOMENT = 0.9
EPS_ADAM = 1e-08
EPS_NORM = 1e-06
LEARN_RATE = 0.5
MESH = pl.DeviceIdType.MESH
F32 = jnp.float32
BF16 = jnp.bfloat16
CHUNKS = 4
SHAPE_ROWS = 512
SPOTS = 8
SPLIT = 1


def kernel(cfg, table_in, g_in, mom_in, sec_in, ls_in, rs_in, lr_in, rr_in, back_arrived, mom, sec, ls, rs, *scratch):
    groups, shards, rb, rows_dev, quarter, block, n, width = cfg
    half = rb // 2
    scratch = list(scratch)

    def take(count):
        got = scratch[:count]
        del scratch[:count]
        return got

    from_next, from_prev, total = take(n), take(n), take(n)
    relay = [take(2) for _ in range(n)]
    (from_opp,) = take(1)
    out_p, arrived = take(n), take(n)
    lr, rr, lroot, rroot, gb, shaped, back, g_ref, table_ref, inv_v, inv_ref = take(11)
    in_sem, g_sem, inv_sem, d_send, d_recv, y_send, y_recv, a_send, a_recv, b_send, b_recv, near_in, line_in, all_in = take(14)

    r, s = lax.axis_index("replica"), lax.axis_index("shard")
    nxt, prv, opp = lax.rem(r + 1, groups), lax.rem(r + groups - 1, groups), lax.rem(r + 2, groups)

    barrier = pltpu.get_barrier_semaphore()
    plane, spot, planes = lax.div(s, SPOTS), lax.rem(s, SPOTS), shards // SPOTS
    in_plane = [(r, plane * SPOTS + lax.rem(spot + k, SPOTS)) for k in range(1, SPOTS)]
    in_line = [(r, lax.rem(plane + k, planes) * SPOTS + spot) for k in range(planes)]
    near = [(nxt, s), (prv, s), (opp, s), in_line[1], in_line[planes - 1]] + in_plane
    def greet(peers):
        for peer in peers:
            pl.semaphore_signal(barrier, inc=1, device_id=peer, device_id_type=MESH)

    greet(near[:3])

    early, late = n - 1, list(range(n - 1))
    spans = [(early * width, width), (0, early * width), (block, quarter - block)]

    def load(i, q, k):
        lo, wide = spans[k]
        at = pl.ds(pl.multiple_of(q * quarter + lo, 128), wide)
        return pltpu.make_async_copy(g_in.at[:, :, at], g_ref.at[:, :, at], g_sem.at[i, k])

    loads = [[load(i, q, k) for k in range(3)] for i, q in enumerate((opp, nxt, prv, r))]
    for i in range(3):
        loads[i][0].start()
    greet(near[3:])
    for i in range(4):
        for k in range(1 if i < 3 else 0, 3):
            loads[i][k].start()
    table_copy = pltpu.make_async_copy(table_in, table_ref, inv_sem.at[0])
    table_copy.start()
    def part(j, c):
        start = c * block + j * width
        return start, max(0, min(width, quarter - start))

    def piece(q, lo, rows, j, c):
        start, wide = part(j, c)
        return g_ref.at[pl.ds(lo, rows), :, pl.ds(pl.multiple_of(q * quarter + start, 128), wide)]

    parts = [(j, c) for j in range(n) for c in range(2) if part(j, c)[1] > 0]
    for j in range(n):
        wide = part(j, 1)[1]
        if wide < width:
            total[j][1, :, :, wide:] = jnp.zeros((rb, rows_dev, width - wide), BF16)
    def y_copy(kind, way, j, c, src, dst):
        return pltpu.make_async_remote_copy(
            src_ref=src,
            dst_ref=dst,
            send_sem=y_send.at[kind, way, j, c],
            recv_sem=y_recv.at[kind, way, j, c],
            device_id=(nxt if way else prv, s),
            device_id_type=MESH,
        )

    first, direct, onward = {}, {}, {}
    for j, c in parts:
        if j == n - 1:
            continue
        wide = pl.ds(0, part(j, c)[1])
        lower, upper = pl.ds(0, half), pl.ds(half, half)
        first[j, c] = [
            y_copy(0, 0, j, c, piece(opp, 0, half, j, c), relay[j][0].at[c, :, :, wide]),
            y_copy(0, 1, j, c, piece(opp, half, half, j, c), relay[j][1].at[c, :, :, wide]),
        ]
        direct[j, c] = [
            y_copy(1, 0, j, c, piece(prv, half, half, j, c), from_next[j].at[c, upper, :, wide]),
            y_copy(1, 1, j, c, piece(nxt, 0, half, j, c), from_prev[j].at[c, lower, :, wide]),
        ]
        onward[j, c] = [
            y_copy(2, 0, j, c, relay[j][0].at[c, :, :, wide], from_next[j].at[c, lower, :, wide]),
            y_copy(2, 1, j, c, relay[j][1].at[c, :, :, wide], from_prev[j].at[c, upper, :, wide]),
        ]

    straight = [
        pltpu.make_async_remote_copy(
            src_ref=piece(q, 0, rb, early, c),
            dst_ref=buf.at[c, :, :, pl.ds(0, part(early, c)[1])],
            send_sem=d_send.at[i, c],
            recv_sem=d_recv.at[i, c],
            device_id=(q, s),
            device_id_type=MESH,
        )
        for i, (q, buf) in enumerate(((opp, from_opp), (nxt, from_prev[early]), (prv, from_next[early])))
        for c in range(2)
        if part(early, c)[1]
    ]

    def start(table, j):
        if j < n:
            for c in range(2):
                for copy in table.get((j, c), ()):
                    copy.start()

    def tell(peers, sem):
        for peer in peers:
            pl.semaphore_signal(sem, inc=1, device_id=peer, device_id_type=MESH)

    for i in range(3):
        loads[i][0].wait()
    pl.semaphore_wait(barrier, len(near))
    tell((in_line[1], in_line[planes - 1]), near_in)
    for copy in straight:
        copy.start()
    for copy in loads[0][1:]:
        copy.wait()
    for j in late:
        start(first, j)
    for copy in loads[1][1:] + loads[2][1:]:
        copy.wait()
    start(direct, 0)
    for copy in loads[3]:
        copy.wait()
    table_copy.wait()
    table = table_ref[pl.ds(r, 1), :]
    rows = lax.broadcasted_iota(jnp.int32, (shards, shards), 0)
    cols = lax.broadcasted_iota(jnp.int32, (shards, shards), 1)
    column = jnp.sum(jnp.where(rows == cols, table, 0), axis=1, keepdims=True)
    inv_v[...] = jnp.zeros_like(inv_v)
    inv_v[:, 0:shards] = jnp.max(jnp.where(column == cols, rows, 0), axis=0, keepdims=True)
    inv_copy = pltpu.make_async_copy(inv_v, inv_ref, inv_sem.at[1])
    inv_copy.start()

    pl.semaphore_wait(near_in, 2)
    tell((in_line[2], in_line[planes - 2]), line_in)
    pl.semaphore_wait(line_in, 2)
    tell(in_plane, all_in)

    in_copies = [
        pltpu.make_async_copy(src, dst, in_sem.at[i])
        for i, (src, dst) in enumerate(((lr_in, lr), (rr_in, rr), (sec_in, sec), (mom_in, mom), (ls_in, ls), (rs_in, rs)))
    ]
    for copy in in_copies:
        copy.start()

    tile = 128

    def mine(q, lo, count, j, c):
        start, wide = part(j, c)
        return g_ref[pl.ds(lo, count), :, pl.ds(pl.multiple_of(q * quarter + start, 128), wide)].astype(F32)

    def pass_on(j):
        for c in range(2):
            wide = part(j, c)[1]
            for way, q, lo in ((0, prv, 0), (1, nxt, half)) if wide else ():
                first[j, c][way].wait_recv()
                buf = relay[j][way]
                buf[c, :, :, 0:wide] = (buf[c, :, :, 0:wide].astype(F32) + mine(q, lo, half, j, c)).astype(BF16)
                onward[j, c][way].start()

    def target(k):
        turn, spot_k = lax.div(k, SPOTS), lax.rem(k, SPOTS)
        far = lax.div(turn + 1, 2)
        off = planes // 2 + far * (1 - 2 * lax.rem(turn, 2))
        return lax.rem(plane + off, planes) * SPOTS + lax.rem(spot + 1 + spot_k, SPOTS)

    def hand_out(j):
        if j == early:
            for copy in straight:
                copy.wait_recv()
        for c in range(2):
            wide = part(j, c)[1]
            if not wide:
                continue
            if j != early:
                for way in range(2):
                    direct[j, c][way].wait_recv()
                    onward[j, c][way].wait_recv()
            summed = mine(r, 0, rb, j, c) + from_next[j][c, :, :, 0:wide].astype(F32) + from_prev[j][c, :, :, 0:wide].astype(F32)
            if j == early:
                summed = summed + from_opp[c, :, :, 0:wide].astype(F32)
            total[j][c, :, :, 0:wide] = summed.astype(BF16)

        def block_of(d):
            b = inv_ref[0, d]
            return total[j][lax.rem(b, 2), lax.div(b, 2)]

        def send(k, carry):
            d = target(k)
            out_p[j][d] = block_of(d)
            pltpu.make_async_remote_copy(
                src_ref=out_p[j].at[d],
                dst_ref=arrived[j].at[s],
                send_sem=a_send.at[j],
                recv_sem=a_recv.at[j],
                device_id=(r, d),
                device_id_type=MESH,
            ).start()
            return carry

        lax.fori_loop(0, shards - 1, send, 0, unroll=9)
        arrived[j][s] = block_of(s)

    def others(src, dst, sem):
        return pltpu.make_async_copy(src.at[pl.ds(0, shards - 1)], dst.at[pl.ds(0, shards - 1)], sem)

    inv_copy.wait()
    for j in late:
        pass_on(j)
        start(direct, j + 1)
        if j == min(1, late[-1]):
            pl.semaphore_wait(all_in, len(in_plane))
            hand_out(early)
    hand_out(0)
    for copy in in_copies[:2]:
        copy.wait()

    def cast_roots(t, carry):
        at = pl.ds(pl.multiple_of(t * tile, tile), tile)
        lroot[at, :] = lr[at, :].astype(BF16)
        rroot[at, :] = rr[at, :].astype(BF16)
        return carry

    lax.fori_loop(0, block // tile, cast_roots, 0)

    for j in late[1:]:
        hand_out(j)

    for copy in in_copies[2:]:
        copy.wait()
    own_c = lax.rem(inv_ref[0, s], 2)
    real = quarter - own_c * block
    chunk_rows = 64
    adam_sq = jnp.zeros((8, width), F32)
    shaped_sq = jnp.zeros((8, block), F32)
    for j in [early] + late:
        others(out_p[j], arrived[j], a_recv.at[j]).wait()
        cols = slice(j * width, (j + 1) * width)

        def second_step(t, acc):
            at = pl.ds(pl.multiple_of(t * chunk_rows, chunk_rows), chunk_rows)
            g = arrived[j][pl.ds(pl.multiple_of(t * (chunk_rows // 8), 8), chunk_rows // 8)].astype(F32).reshape(chunk_rows, width)
            gb[at, cols] = g.astype(BF16)
            second = BETA_SECOND * sec[at, cols] + (1.0 - BETA_SECOND) * g * g
            sec[at, cols] = second
            adam = g / (jnp.sqrt(second) + EPS_ADAM)
            return acc + jnp.sum((adam * adam).reshape(chunk_rows // 8, 8, width), axis=0)

        adam_sq = lax.fori_loop(0, block // chunk_rows, second_step, adam_sq, unroll=True)

        def shape_step(t, acc):
            at = pl.ds(pl.multiple_of(t * SHAPE_ROWS, SHAPE_ROWS), SHAPE_ROWS)
            left = jnp.dot(lroot[at, :], gb[:, cols], preferred_element_type=F32).astype(BF16)
            both = jnp.dot(left, rroot[cols, :], preferred_element_type=F32)
            if j != early:
                both = both + shaped[at, :]
            if j == late[-1]:
                both = jnp.where(lax.broadcasted_iota(jnp.int32, (SHAPE_ROWS, block), 1) < real, both, 0.0)
                acc = acc + jnp.sum((both * both).reshape(SHAPE_ROWS // 8, 8, block), axis=0)
            shaped[at, :] = both
            return acc

        shaped_sq = lax.fori_loop(0, block // SHAPE_ROWS, shape_step, shaped_sq, unroll=True)

    adam_norm = jnp.sum(jnp.sum(adam_sq, axis=0, keepdims=True), axis=1, keepdims=True)
    shaped_norm = jnp.sum(jnp.sum(shaped_sq, axis=0, keepdims=True), axis=1, keepdims=True)
    scale = jnp.sqrt(adam_norm + EPS_NORM) / jnp.sqrt(shaped_norm + EPS_NORM)

    per = chunk_rows // 8
    turns = shards // per

    def send_back(d):
        pltpu.make_async_remote_copy(
            src_ref=back.at[d],
            dst_ref=back_arrived.at[s],
            send_sem=b_send,
            recv_sem=b_recv,
            device_id=(r, d),
            device_id_type=MESH,
        ).start()

    for k in range(turns):
        far = (k + 1) // 2
        t = lax.rem(lax.div(s, per) + turns // 2 + (-far if k % 2 else far), turns)
        at = pl.ds(pl.multiple_of(t * chunk_rows, chunk_rows), chunk_rows)
        moment = BETA_MOMENT * mom[at, :] + scale * shaped[at, :]
        mom[at, :] = moment
        back[pl.ds(pl.multiple_of(t * per, per), per)] = (-LEARN_RATE * moment).reshape(per, 8, block).astype(BF16)
        last = k == turns - 1
        for i in range(per - 1 if last else per):
            send_back(t * per + (lax.rem(s + 1 + i, per) if last else i))

    back_arrived[s] = back[s]

    def left_step(t, carry):
        at = pl.ds(pl.multiple_of(t * tile, tile), tile)
        gram = lax.dot_general(gb[at, :], gb[...], (((1,), (1,)), ((), ())), preferred_element_type=F32)
        ls[at, :] = BETA_STAT * ls[at, :] + (1.0 - BETA_STAT) * gram
        return carry

    lax.fori_loop(0, block // tile, left_step, 0)

    for t in range(block // tile):
        at = slice(t * tile, (t + 1) * tile)
        gram = lax.dot_general(gb[:, at], gb[...], (((0,), (0,)), ((), ())), preferred_element_type=F32)
        rs[at, :] = BETA_STAT * rs[at, :] + (1.0 - BETA_STAT) * gram

    others(back, back_arrived, b_recv).wait()

    for copy in straight:
        copy.wait_send()
    for table in (first, direct, onward):
        for pair in table.values():
            for copy in pair:
                copy.wait_send()
    for j in range(n):
        others(out_p[j], arrived[j], a_send.at[j]).wait()
    others(back, back_arrived, b_send).wait()


def finish(quarter, block, table_in, arrived, mom, sec, ls, rs, upd_out, mom_out, sec_out, left_out, right_out, upd, table_ref, sem, table_sem):
    table_copy = pltpu.make_async_copy(table_in, table_ref, table_sem)
    table_copy.start()
    pairs = ((mom, mom_out), (sec, sec_out), (ls, left_out), (rs, right_out))
    rows = block // SPLIT
    copies = [
        pltpu.make_async_copy(src.at[pl.ds(k * rows, rows)], dst.at[pl.ds(k * rows, rows)], sem.at[i * SPLIT + k])
        for i, (src, dst) in enumerate(pairs)
        for k in range(SPLIT)
    ]
    for copy in copies:
        copy.start()

    r = lax.axis_index("replica")
    table_copy.wait()

    def place(i, carry):
        upd[i, :, 0:block] = arrived[table_ref[r, 2 * i]]
        upd[i, :, block:quarter] = arrived[table_ref[r, 2 * i + 1]][:, 0 : quarter - block]
        return carry

    lax.fori_loop(0, upd.shape[0], place, 0)
    last = pltpu.make_async_copy(upd, upd_out, sem.at[4 * SPLIT])
    last.start()
    for copy in copies:
        copy.wait()
    last.wait()


def per_device(grads, owner_table, momentum, second, left_stat, right_stat, left_root, right_root):
    groups, shards = lax.axis_size("replica"), lax.axis_size("shard")
    _, rb, rows_dev, full_width = grads.shape
    block = left_stat.shape[2]
    quarter = full_width // groups
    n = CHUNKS
    width = block // n
    cfg = (groups, shards, rb, rows_dev, quarter, block, n, width)
    sq = (block, block)
    whole = pltpu.VMEM((2, rb, rows_dev, width), BF16)
    halves = pltpu.VMEM((2, rb // 2, rows_dev, width), BF16)
    slots = pltpu.VMEM((shards, rows_dev, width), BF16)
    wide_slots = pltpu.VMEM((shards, rows_dev, block), BF16)
    dma = pltpu.SemaphoreType.DMA
    hbm = pl.BlockSpec(memory_space=pltpu.HBM)
    vmem = pl.BlockSpec(memory_space=pltpu.VMEM)
    operands = (owner_table, grads[0], *[a[0, 0] for a in (momentum, second, left_stat, right_stat, left_root, right_root)])
    results = pl.pallas_call(
        functools.partial(kernel, cfg),
        name="shampoo_step",
        out_shape=(pltpu.VMEM((shards, rows_dev, block), BF16),) + (pltpu.VMEM(sq, F32),) * 4,
        in_specs=[hbm] * 8,
        out_specs=[vmem] * 5,
        scratch_shapes=[whole] * (3 * n)
        + [halves] * (2 * n)
        + [whole]
        + [slots] * (2 * n)
        + [pltpu.VMEM(sq, F32)] * 2
        + [pltpu.VMEM(sq, BF16)] * 3
        + [pltpu.VMEM(sq, F32), wide_slots, pltpu.VMEM((rb, rows_dev, full_width), BF16)]
        + [pltpu.VMEM(owner_table.shape, jnp.int32), pltpu.VMEM((1, 128), jnp.int32), pltpu.SMEM((1, 128), jnp.int32)]
        + [dma((6,)), dma((4, 3)), dma((2,)), dma((3, 2)), dma((3, 2)), dma((3, 2, n, 2)), dma((3, 2, n, 2)), dma((n,)), dma((n,)), dma, dma] + [pltpu.SemaphoreType.REGULAR] * 3,
        compiler_params=pltpu.CompilerParams(collective_id=1, has_side_effects=True, vmem_limit_bytes=40 * 2**20),
        cost_estimate=pl.CostEstimate(flops=8 * block**3, bytes_accessed=16 * 2**20, transcendentals=0),
    )(*[pltpu.with_memory_space_constraint(a, pltpu.HBM) for a in operands])
    update, moment_new, second_new, left_new, right_new = pl.pallas_call(
        functools.partial(finish, quarter, block),
        name="place_update",
        out_shape=(jax.ShapeDtypeStruct((rb, rows_dev, quarter), BF16),) + (jax.ShapeDtypeStruct(sq, F32),) * 4,
        in_specs=[hbm] + [vmem] * 5,
        out_specs=[hbm] * 5,
        scratch_shapes=[pltpu.VMEM((rb, rows_dev, quarter), BF16), pltpu.SMEM(owner_table.shape, jnp.int32), dma((4 * SPLIT + 1,)), dma],
        compiler_params=pltpu.CompilerParams(vmem_limit_bytes=8 * 2**20),
    )(pltpu.with_memory_space_constraint(owner_table, pltpu.HBM), *results)
    shape_own = (1, 1, block, block)
    return (
        update,
        moment_new.reshape(shape_own),
        second_new.reshape(shape_own),
        left_new.reshape(shape_own),
        right_new.reshape(shape_own),
    )


def solution(mesh):
    owned = P("replica", "shard", None, None)
    return jax.shard_map(
        per_device,
        mesh=mesh,
        in_specs=(P("replica", None, "shard", None), P(), owned, owned, owned, owned, owned, owned),
        out_specs=(P(None, "shard", "replica"), owned, owned, owned, owned),
        check_vma=False,
    )
```
